32 devices in a mesh: gx: 8 (over z, y), gy: 4 (over x, core).
Axes of the slice: x: 2, y: 2, z: 4, core: 2. Of those that a mesh axis runs over, the one named last changes fastest.
Arguments:
- gas_moisture: float32 [16, 512, 512], P(None, 'gx', 'gy'), may hold values from 0 to 1
- gas_warmth: float32 [16, 512, 512], P(None, 'gx', 'gy'), may hold values from 0.5 to 1.5
- prior_moisture: float32 [16, 512, 512], P(None, 'gx', 'gy'), may hold values from 0 to 1
- prior_warmth: float32 [16, 512, 512], P(None, 'gx', 'gy'), may hold values from 0.5 to 1.5
- flow_speeds: bfloat16 [3, 16, 512, 512], P(None, None, 'gx', 'gy'), may hold values from -4 to 4
- lower_base_cell: int32 [3, 4, 32768], P(None, 'gy', 'gx'), may hold values from 0 to 510, as said below
- trilinear_factors: float32 [8, 4, 32768], P(None, 'gy', 'gx'), may hold values from 0.02 to 0.25
- panel_surface: float32 [4, 32768], P('gy', 'gx'), may hold values from 0.3 to 9
- panel_owner: int32 [4, 32768], P('gy', 'gx'), may hold values from 0 to 159, as said below
- active_panel_tally: int32 [4, 8], P('gy', 'gx'), may hold values from 512 to 4096, as said below
Outputs:
- following_moisture: float32 [16, 512, 512], P(None, 'gx', 'gy')
- following_warmth: float32 [16, 512, 512], P(None, 'gx', 'gy')
The draws below stay inside these ranges and needn't reach their ends.
Inputs may be any that keep to these rules, and one draw needn't show every extreme that they name: lower_base_cell[0] is a plane of the slab; lower_base_cell[1] lies in the block of 64 cells of the element's gx index, at most 62 past its start; lower_base_cell[2] lies in the block of 128 cells of the element's group, at most 126 past its start. `panel_owner`: every droplet number of a group is named by a live element of that group's row. `active_panel_tally`: every row has a block with exactly 4096 live elements.
All inputs are finite; a program needn't handle non-finite values.
Results may differ from the reference program's by a relative error of at most 0.0003.
Values sent between devices are 32-bit elements; how exact they have to be, the bound alone decides.
No kernel may reach another device: no remote copies, remote signals or barrier semaphores. Data moves between devices by JAX's collectives and lax.ppermute only.
A program may use at most 128 MiB of HBM per device.

```python
import jax
import jax.numpy as jnp

MESH_FIRST_AXIS = 16
CX = 64
CY = 128
FE = 4096
DROP_DEV = 20
SLABS = 8
DROP_GROUPS = 4
MESH_SECOND_AXIS = 512
MESH_THIRD_AXIS = 512
SURFACE_SLOTS = 32768
DROPS = 160


def draw_lower_base_cell(key, part):
    first, second, third = jax.random.split(key, 3)
    slots = jnp.arange(SURFACE_SLOTS)[None, :]
    groups = jnp.arange(DROP_GROUPS)[:, None]
    position = slots % FE
    row_offset = jax.random.randint(first, (DROP_GROUPS, SURFACE_SLOTS), 0, CX - 1)
    col_offset = jax.random.randint(second, (DROP_GROUPS, SURFACE_SLOTS), 0, CY - 1)
    planes_at = jax.random.randint(third, (DROP_GROUPS, SURFACE_SLOTS), 0, MESH_FIRST_AXIS)
    row_offset = jnp.where(position == 0, 0, jnp.where(position == FE - 1, CX - 2, row_offset))
    col_offset = jnp.where(position == 0, 0, jnp.where(position == FE - 1, CY - 2, col_offset))
    planes_at = jnp.where(position == 0, 0, jnp.where(position == FE - 1, MESH_FIRST_AXIS - 1, planes_at))
    rows_at = slots // FE * CX + row_offset
    cols_at = groups * CY + col_offset
    return jnp.stack([planes_at, rows_at, cols_at]).astype(jnp.int32)


def draw_active_panel_tally(key, part):
    first, second = jax.random.split(key)
    spread = jax.random.randint(first, (DROP_GROUPS, SLABS), 0, 65)
    counts = FE // 8 + (FE - FE // 8) * spread * spread // 4096
    fullest = jax.random.randint(second, (DROP_GROUPS, 1), 0, SLABS)
    counts = jnp.where(jnp.arange(SLABS)[None, :] == fullest, FE, counts)
    return counts.astype(jnp.int32)


def draw_panel_owner(key, part):
    slots = jnp.arange(SURFACE_SLOTS)[None, :]
    position = slots % FE
    blocks = slots // FE
    random_ids = jax.random.randint(key, (DROP_GROUPS, SURFACE_SLOTS), 0, DROPS)
    return jnp.where(position < DROP_DEV, blocks * DROP_DEV + position, random_ids).astype(jnp.int32)


def draw_panel_surface(key, part):
    blocks = (jnp.arange(SURFACE_SLOTS) // FE).astype(jnp.float32)[None, :]
    ramp = 1.0 + 2.0 * blocks / max(SLABS - 1, 1)
    base = jax.random.uniform(key, (DROP_GROUPS, SURFACE_SLOTS), jnp.float32, 0.5, 1.5)
    return (base * ramp).astype(jnp.float32)


def shard_levels(own_key, extent, shards, smallest, largest):
    def one(dim, shards_of):
        draws = jax.random.uniform(jax.random.fold_in(jax.random.fold_in(own_key, 6), dim), (shards_of,), jnp.float32, smallest / len(shards), largest / len(shards))
        return jnp.repeat(jnp.exp(draws), extent[dim] // shards_of).reshape((-1,) + (1,) * (len(extent) - dim - 1))

    factor_of = one(*shards[0])
    for cut in shards[1:]:
        factor_of = factor_of * one(*cut)
    return factor_of


def noise(own_key, shape, scale, reach, cuts=(), kind=jnp.bfloat16):
    gain = shard_levels(own_key, shape, cuts, -0.22, 0.18) if cuts else 1.0
    drawn = jax.random.normal(own_key, shape, jnp.float32) * scale * gain
    return jnp.minimum(jnp.maximum(drawn, -reach), reach).astype(kind)


def setup_inputs(seed: int = 0) -> dict:
    keys = jax.random.split(jax.random.key(seed), 11)
    return {
        "gas_moisture": jnp.clip(1.0 * jax.random.uniform(keys[0], (MESH_FIRST_AXIS, MESH_SECOND_AXIS, MESH_THIRD_AXIS), jnp.float32) ** shard_levels(keys[0], (MESH_FIRST_AXIS, MESH_SECOND_AXIS, MESH_THIRD_AXIS), ((1, 8), (2, 4)), -0.2, 0.2), 0.0, 1.0),
        "gas_warmth": jnp.clip(0.5 + 1.0 * jax.random.uniform(keys[1], (MESH_FIRST_AXIS, MESH_SECOND_AXIS, MESH_THIRD_AXIS), jnp.float32) ** shard_levels(keys[1], (MESH_FIRST_AXIS, MESH_SECOND_AXIS, MESH_THIRD_AXIS), ((1, 8), (2, 4)), -0.2, 0.2), 0.5, 1.5),
        "prior_moisture": jnp.clip(1.0 * jax.random.uniform(keys[2], (MESH_FIRST_AXIS, MESH_SECOND_AXIS, MESH_THIRD_AXIS), jnp.float32) ** shard_levels(keys[2], (MESH_FIRST_AXIS, MESH_SECOND_AXIS, MESH_THIRD_AXIS), ((1, 8), (2, 4)), -0.2, 0.2), 0.0, 1.0),
        "prior_warmth": jnp.clip(0.5 + 1.0 * jax.random.uniform(keys[3], (MESH_FIRST_AXIS, MESH_SECOND_AXIS, MESH_THIRD_AXIS), jnp.float32) ** shard_levels(keys[3], (MESH_FIRST_AXIS, MESH_SECOND_AXIS, MESH_THIRD_AXIS), ((1, 8), (2, 4)), -0.2, 0.2), 0.5, 1.5),
        "flow_speeds": noise(keys[4], (3, MESH_FIRST_AXIS, MESH_SECOND_AXIS, MESH_THIRD_AXIS), 1.0, 4.0, ((2, 8), (3, 4))),
        "lower_base_cell": draw_lower_base_cell(jax.random.fold_in(keys[10], 71), 0),
        "trilinear_factors": jnp.clip(0.02 + 0.23 * jax.random.uniform(keys[6], (8, DROP_GROUPS, SURFACE_SLOTS), jnp.float32) ** shard_levels(keys[6], (8, DROP_GROUPS, SURFACE_SLOTS), ((1, 4), (2, 8)), -0.2, 0.2), 0.02, 0.25),
        "panel_surface": draw_panel_surface(jax.random.fold_in(keys[10], 71), 0),
        "panel_owner": draw_panel_owner(jax.random.fold_in(keys[10], 71), 0),
        "active_panel_tally": draw_active_panel_tally(jax.random.fold_in(keys[10], 71), 0),
    }


OFFSETS = ((0, 0, 0), (0, 0, 1), (0, 1, 0), (0, 1, 1), (1, 0, 0), (1, 0, 1), (1, 1, 0), (1, 1, 1))
increment_span = 0.1
diffusivity = 1.0
mass_rate = 2.0
saturation_rate = 2.0
thermal_flux = 1.0
enthalpy_evaporation = 0.5


def derivative_value(field, flow_speeds):
    total = jnp.zeros_like(field)
    for axis_number in range(3):
        ahead_one = jnp.roll(field, -1, axis_number)
        ahead_two = jnp.roll(field, -2, axis_number)
        behind_one = jnp.roll(field, 1, axis_number)
        behind_two = jnp.roll(field, 2, axis_number)
        slope = (8.0 * (ahead_one - behind_one) - (ahead_two - behind_two)) / 12.0
        curve = (16.0 * (ahead_one + behind_one) - (ahead_two + behind_two) - 30.0 * field) / 12.0
        total = total - flow_speeds[axis_number].astype(jnp.float32) * slope + diffusivity * curve
    return total


def reference(gas_moisture, gas_warmth, prior_moisture, prior_warmth, flow_speeds, lower_base_cell, trilinear_factors, panel_surface, panel_owner, active_panel_tally):
    column_ids = jnp.arange(DROP_GROUPS).astype(jnp.int32)[:, None]
    slots = jnp.arange(SURFACE_SLOTS).astype(jnp.int32)[None, :]
    owners = jnp.broadcast_to(slots // FE, (DROP_GROUPS, SURFACE_SLOTS)).astype(jnp.int32)
    live_count = jnp.take_along_axis(active_panel_tally, owners, axis=1)
    living = (slots % FE) < live_count
    moist_surface = jnp.where(living, panel_surface, jnp.zeros_like(panel_surface))
    moisture_panels = jnp.zeros((DROP_GROUPS, SURFACE_SLOTS), jnp.float32)
    panel_warmth = jnp.zeros((DROP_GROUPS, SURFACE_SLOTS), jnp.float32)
    cells = []
    for panel_ordinal, corner in enumerate(OFFSETS):
        first_axis_position = (lower_base_cell[0] + corner[0]) % MESH_FIRST_AXIS
        second_axis_position = lower_base_cell[1] + corner[1]
        group_position = lower_base_cell[2] + corner[2]
        cells.append((first_axis_position, second_axis_position, group_position))
        moisture_panels = moisture_panels + trilinear_factors[panel_ordinal] * gas_moisture[first_axis_position, second_axis_position, group_position]
        panel_warmth = panel_warmth + trilinear_factors[panel_ordinal] * gas_warmth[first_axis_position, second_axis_position, group_position]
    partition_label = (column_ids * DROPS + panel_owner).astype(jnp.int32)
    summands = jnp.stack([moist_surface, moist_surface * moisture_panels, moist_surface * panel_warmth], axis=-1).reshape(-1, 3)
    sums = jax.ops.segment_sum(summands, partition_label.reshape(-1), num_segments=DROP_GROUPS * DROPS)
    drop_vapour = sums[:, 1] / sums[:, 0]
    particle_warmth = sums[:, 2] / sums[:, 0]
    saturated = 0.5 * jnp.exp(saturation_rate * (particle_warmth - 1.0))
    evaporated_amount = mass_rate * moist_surface * (jnp.take(saturated, partition_label) - 0.5 * (jnp.take(drop_vapour, partition_label) + moisture_panels))
    thermal_energy = moist_surface * thermal_flux * (jnp.take(particle_warmth, partition_label) - panel_warmth) - enthalpy_evaporation * evaporated_amount
    vap_source = jnp.zeros((MESH_FIRST_AXIS, MESH_SECOND_AXIS, MESH_THIRD_AXIS), jnp.float32)
    warmth_forcing = jnp.zeros((MESH_FIRST_AXIS, MESH_SECOND_AXIS, MESH_THIRD_AXIS), jnp.float32)
    for panel_ordinal, (first_axis_position, second_axis_position, group_position) in enumerate(cells):
        vap_source = vap_source.at[first_axis_position, second_axis_position, group_position].add(trilinear_factors[panel_ordinal] * evaporated_amount)
        warmth_forcing = warmth_forcing.at[first_axis_position, second_axis_position, group_position].add(trilinear_factors[panel_ordinal] * thermal_energy)
    following_moisture = gas_moisture + increment_span * (1.5 * derivative_value(gas_moisture, flow_speeds) - 0.5 * derivative_value(prior_moisture, flow_speeds)) + vap_source
    following_warmth = gas_warmth + increment_span * (1.5 * derivative_value(gas_warmth, flow_speeds) - 0.5 * derivative_value(prior_warmth, flow_speeds)) + warmth_forcing
    return following_moisture, following_warmth
```

```python
import functools

import jax
import jax.numpy as jnp
from jax import lax
from jax.experimental import pallas as pl
from jax.experimental.pallas import tpu as pltpu
from jax.sharding import PartitionSpec as P

DROP_DEV = 20
LANES = 128
HALF = 64

increment_span = 0.1
diffusivity = 1.0
mass_rate = 2.0
saturation_rate = 2.0
thermal_flux = 1.0
enthalpy_evaporation = 0.5

VMEM = pl.BlockSpec(memory_space=pltpu.VMEM)
SMEM = pl.BlockSpec(memory_space=pltpu.SMEM)
COPIES = 4


def iota(shape, dim):
    return lax.broadcasted_iota(jnp.int32, shape, dim)


def pick(values, index):
    return jnp.take_along_axis(values, index, axis=1, mode="promise_in_bounds")


def swap_rows(x, even):
    return jnp.where(even, pltpu.roll(x, 7, 0), pltpu.roll(x, 1, 0))


def edges_kernel(moist, warm, old_moist, old_warm, blend, top, bottom, left, right):
    planes, rows, cols = moist.shape
    for field, (now, old) in enumerate(((moist, old_moist), (warm, old_warm))):
        for pair in range(planes // 2):
            halves = []
            for plane in (2 * pair, 2 * pair + 1):
                mixed = 1.5 * now[plane] - 0.5 * old[plane]
                blend[field, plane] = mixed
                top[field, plane] = mixed[0:2]
                bottom[field, plane] = mixed[rows - 2 : rows]
                halves.append(mixed)
            turned = jnp.concatenate(halves, axis=0).T
            at = (field * planes // 2 + pair) * 2 * rows
            left[:, pl.ds(at, 2 * rows)] = turned[0:2]
            right[:, pl.ds(at, 2 * rows)] = turned[cols - 2 : cols]


def gather_kernel(index, tally, moist, warm, factors, surface, owner, scaled, fronts, sums, table, terms):
    planes, rows, cols = moist.shape
    groups = surface.shape[0]
    drops = sums.shape[1]
    for plane in range(planes):
        below = (plane - 1) % planes
        table[pl.ds(plane * rows * 4, rows, stride=4), :] = moist[plane]
        table[pl.ds(plane * rows * 4 + 1, rows, stride=4), :] = warm[plane]
        table[pl.ds(below * rows * 4 + 2, rows, stride=4), :] = moist[plane]
        table[pl.ds(below * rows * 4 + 3, rows, stride=4), :] = warm[plane]
    live = tally[0, 0]

    def group_step(group, carry):
        lane = iota((8, LANES), 1)
        sub = iota((8, LANES), 0)
        even = (sub & 1) == 0
        even_lane = (lane & 1) == 0
        raw = factors[pl.ds(group, 8, stride=groups), :]
        raw = jnp.where(
            (sub == 2) | (sub == 3),
            pltpu.roll(raw, 6, 0),
            jnp.where((sub == 4) | (sub == 5), pltpu.roll(raw, 2, 0), raw),
        )
        area = jnp.broadcast_to(surface[pl.ds(group, 1), :], (8, LANES))
        area = jnp.where(lane + group * LANES < live, area, 0.0)
        values = []
        for half in range(2):
            found = jnp.zeros((8, LANES), jnp.float32)
            for j in range(HALF):
                word = index[group * LANES + half * HALF + j]
                row = lax.shift_right_logical(word, 7)
                entry = table[pl.ds(row * 4, 8), :]
                entry = pltpu.roll(entry, word & 127, 1)
                found = jnp.where(lane >= 2 * j, entry, found)
            spread = (lane >> 1) + half * HALF
            weight = pick(raw, spread)
            weight = jnp.where((lane & 1) == (sub & 1), weight, swap_rows(weight, even))
            value = found * weight
            value = value + pltpu.roll(value, 2, 0)
            value = value + pltpu.roll(value, 4, 0)
            value = value + jnp.where(even_lane, pltpu.roll(value, 127, 1), pltpu.roll(value, 1, 1))
            at = pl.ds((group * 2 + half) * 8, 8)
            scaled[at, :] = weight * pick(area, spread)
            fronts[at, :] = jnp.where(even, value, value - 0.5 * swap_rows(value, even))
            values.append(pick(value, (lane * 2) & 127))
        value = jnp.where(lane < HALF, values[0], values[1])
        term = jnp.where(sub == 2, 1.0, value) * area
        high = term.astype(jnp.bfloat16).astype(jnp.float32)
        both = jnp.concatenate([high, term - high], axis=0).astype(jnp.bfloat16)
        terms[:, pl.ds(pl.multiple_of(group * LANES, LANES), LANES)] = both
        return carry

    lax.fori_loop(0, groups, group_step, 0)
    total = jnp.zeros((16, drops), jnp.float32)
    span = 8
    for first in range(0, groups, span):
        tables = []
        for group in range(first, first + span):
            label = jnp.broadcast_to(owner[pl.ds(group, 1), :], (drops, LANES))
            tables.append((label == iota((drops, LANES), 0)).astype(jnp.float32).astype(jnp.bfloat16))
        total = total + lax.dot_general(
            terms[:, first * LANES : (first + span) * LANES],
            jnp.concatenate(tables, axis=1),
            (((1,), (1,)), ((), ())),
            preferred_element_type=jnp.float32,
        )
    sums[...] = total[0:8] + total[8:16]


def stencil_kernel(blend, moist, warm, speed, above, below, left, right, out_moist, out_warm, padded, side):
    planes, rows, cols = moist.shape
    for field in range(2):
        for plane in range(planes):
            padded[field, plane, 8 : rows + 8, :] = blend[field, plane]
            padded[field, plane, 6:8, :] = above[field, plane]
            padded[field, plane, rows + 8 : rows + 10, :] = below[field, plane]
        for pair in range(planes // 2):
            slot = field * (planes // 2) + pair
            at = slot * 2 * rows
            block = jnp.concatenate(
                [
                    right[:, pl.ds(at, 2 * rows)],
                    jnp.zeros((cols - 4, 2 * rows), jnp.float32),
                    left[:, pl.ds(at, 2 * rows)],
                ],
                axis=0,
            )
            side[pl.ds(slot * 2 * rows, 2 * rows), :] = block.T
    lane = iota((rows, cols), 1)
    fraction = increment_span / 12.0

    def plane_step(plane, carry):
        speeds = [speed[k, plane].astype(jnp.float32) * fraction for k in range(3)]
        for field, (now, out) in enumerate(((moist, out_moist), (warm, out_warm))):
            center = padded[field, plane, 8 : rows + 8, :]
            edge = side[pl.ds(pl.multiple_of((field * planes + plane) * rows, rows), rows), :]
            wrap = lambda shift: padded[field, lax.rem(plane + shift + planes, planes), 8 : rows + 8, :]
            shift = lambda by: padded[field, plane, 8 + by : rows + 8 + by, :]
            around = [
                (wrap(1), wrap(2), wrap(-1), wrap(-2)),
                (shift(1), shift(2), shift(-1), shift(-2)),
                (
                    pltpu.roll(jnp.where(lane < 1, edge, center), cols - 1, 1),
                    pltpu.roll(jnp.where(lane < 2, edge, center), cols - 2, 1),
                    pltpu.roll(jnp.where(lane >= cols - 1, edge, center), 1, 1),
                    pltpu.roll(jnp.where(lane >= cols - 2, edge, center), 2, 1),
                ),
            ]
            near = 0.0
            far = 0.0
            total = now[plane] - (90.0 * diffusivity * fraction) * center
            for k, (ahead_one, ahead_two, behind_one, behind_two) in enumerate(around):
                near = near + (ahead_one + behind_one)
                far = far + (ahead_two + behind_two)
                total = total - speeds[k] * (8.0 * (ahead_one - behind_one) - (ahead_two - behind_two))
            out[plane] = total + (diffusivity * fraction) * (16.0 * near - far)
        return carry

    lax.fori_loop(0, planes, plane_step, 0)


def scatter_kernel(index, scaled, fronts, owner, sums, start_moist, start_warm, out_moist, out_warm, *banks):
    planes, rows, cols = start_moist.shape
    groups = owner.shape[0]
    drops = sums.shape[1]
    size = banks[0].shape[0]

    def clear(step, carry):
        for bank in banks:
            bank[pl.ds(pl.multiple_of(step * 128, 128), 128), :] = jnp.zeros((128, cols), jnp.float32)
        return carry

    lax.fori_loop(0, size // 128, clear, 0)
    totals = sums[...]
    drop_vapour = totals[0:1] / totals[2:3]
    drop_warmth = totals[1:2] / totals[2:3]
    saturated = 0.5 * jnp.exp(saturation_rate * (drop_warmth - 1.0))
    for_mass = 2.0 * saturated - drop_vapour
    for_heat = drop_warmth - 0.5 * for_mass
    wide = (8, drops)
    both = jnp.where(
        (iota(wide, 0) & 1) == 0, jnp.broadcast_to(for_mass, wide), jnp.broadcast_to(for_heat, wide)
    )
    pieces = []
    for at in range(0, drops, LANES):
        piece = both[:, at : min(at + LANES, drops)]
        if piece.shape[1] < LANES:
            piece = jnp.concatenate([piece, jnp.zeros((8, LANES - piece.shape[1]), jnp.float32)], axis=1)
        pieces.append(piece)

    def group_step(group, carry):
        lane = iota((8, LANES), 1)
        label = jnp.broadcast_to(owner[pl.ds(group, 1), :], (8, LANES))
        looked = pick(pieces[0], label & 127)
        for number in range(1, len(pieces)):
            looked = jnp.where(label >= number * LANES, pick(pieces[number], label & 127), looked)
        for half in range(2):
            at = pl.ds((group * 2 + half) * 8, 8)
            value = scaled[at, :] * (pick(looked, (lane >> 1) + half * HALF) - fronts[at, :])
            for j in range(HALF):
                word = index[group * LANES + half * HALF + j]
                row = lax.shift_right_logical(word, 7)
                entry = jnp.where((lane >> 1) == j, value, 0.0)
                entry = pltpu.roll(entry, (128 - word) & 127, 1)
                banks[j % len(banks)][pl.ds(row * 4, 8), :] += entry
        return carry

    lax.fori_loop(0, groups, group_step, 0)
    for plane in range(planes):
        before = (plane - 1) % planes
        for field, (start, out) in enumerate(((start_moist, out_moist), (start_warm, out_warm))):
            total = start[plane]
            for bank in banks:
                total = total + bank[pl.ds(plane * rows * 4 + field, rows, stride=4), :]
                total = total + bank[pl.ds(before * rows * 4 + 2 + field, rows, stride=4), :]
            out[plane] = total


def params(megabytes=40):
    return pltpu.CompilerParams(vmem_limit_bytes=megabytes << 20)


def shards(
    gas_moisture,
    gas_warmth,
    prior_moisture,
    prior_warmth,
    flow_speeds,
    lower_base_cell,
    trilinear_factors,
    panel_surface,
    panel_owner,
    active_panel_tally,
):
    planes, rows, cols = gas_moisture.shape
    drops = DROP_DEV * lax.axis_size("gx")
    count = panel_surface.shape[1]
    groups = count // LANES
    f32 = jnp.float32
    shape = jax.ShapeDtypeStruct
    row_local = lower_base_cell[1, 0] - lax.axis_index("gx") * rows
    col_local = lower_base_cell[2, 0] - lax.axis_index("gy") * cols
    turn = (2 * (jnp.arange(count, dtype=jnp.int32) % HALF) - col_local) & 127
    index = (lower_base_cell[0, 0] * rows + row_local) * 128 + turn
    factors = trilinear_factors.reshape(8 * groups, LANES)
    surface = panel_surface.reshape(groups, LANES)
    owner = panel_owner.reshape(groups, LANES)
    field = shape((planes, rows, cols), f32)

    blend, top, bottom, left, right = pl.pallas_call(
        edges_kernel,
        out_shape=(
            shape((2, planes, rows, cols), f32),
            shape((2, planes, 2, cols), f32),
            shape((2, planes, 2, cols), f32),
            shape((2, 2 * planes * rows), f32),
            shape((2, 2 * planes * rows), f32),
        ),
        in_specs=[VMEM] * 4,
        out_specs=[VMEM] * 5,
        compiler_params=params(),
        name="edges",
    )(gas_moisture, gas_warmth, prior_moisture, prior_warmth)

    def around(axis, head, tail):
        size = lax.axis_size(axis)
        onward = [(i, (i + 1) % size) for i in range(size)]
        backward = [((i + 1) % size, i) for i in range(size)]
        return lax.ppermute(tail, axis, onward), lax.ppermute(head, axis, backward)

    above, below = around("gx", top, bottom)
    from_left, from_right = around("gy", left, right)

    scaled, fronts, sums = pl.pallas_call(
        gather_kernel,
        out_shape=(
            shape((2 * groups * 8, LANES), f32),
            shape((2 * groups * 8, LANES), f32),
            shape((8, drops), f32),
        ),
        in_specs=[SMEM, SMEM] + [VMEM] * 5,
        out_specs=[VMEM] * 3,
        scratch_shapes=[
            pltpu.VMEM((planes * rows * 4 + 8, cols), f32),
            pltpu.VMEM((16, count), jnp.bfloat16),
        ],
        compiler_params=params(),
        name="gather",
    )(index, active_panel_tally, gas_moisture, gas_warmth, factors, surface, owner)

    totals = lax.psum(sums, "gx")

    start_moist, start_warm = pl.pallas_call(
        stencil_kernel,
        out_shape=(field, field),
        in_specs=[VMEM] * 8,
        out_specs=[VMEM] * 2,
        scratch_shapes=[
            pltpu.VMEM((2, planes, rows + 16, cols), f32),
            pltpu.VMEM((2 * planes * rows, cols), f32),
        ],
        compiler_params=params(),
        name="stencil",
    )(blend, gas_moisture, gas_warmth, flow_speeds, above, below, from_left, from_right)

    size = planes * rows * 4 + 128
    return pl.pallas_call(
        scatter_kernel,
        out_shape=(field, field),
        in_specs=[SMEM] + [VMEM] * 6,
        out_specs=[VMEM] * 2,
        scratch_shapes=[pltpu.VMEM((size, cols), f32)] * COPIES,
        compiler_params=params(),
        name="scatter",
    )(index, scaled, fronts, owner, totals, start_moist, start_warm)


def solution(mesh):
    return jax.shard_map(
        shards,
        mesh=mesh,
        in_specs=(
            P(None, "gx", "gy"),
            P(None, "gx", "gy"),
            P(None, "gx", "gy"),
            P(None, "gx", "gy"),
            P(None, None, "gx", "gy"),
            P(None, "gy", "gx"),
            P(None, "gy", "gx"),
            P("gy", "gx"),
            P("gy", "gx"),
            P("gy", "gx"),
        ),
        out_specs=(P(None, "gx", "gy"), P(None, "gx", "gy")),
        check_vma=False,
    )
```

```python
import functools

import jax
import jax.numpy as jnp
from jax import lax
from jax.experimental import pallas as pl
from jax.experimental.pallas import tpu as pltpu
from jax.sharding import PartitionSpec as P

DROP_DEV = 20
LANES = 128
HALF = 64

increment_span = 0.1
diffusivity = 1.0
mass_rate = 2.0
saturation_rate = 2.0
thermal_flux = 1.0
enthalpy_evaporation = 0.5

VMEM = pl.BlockSpec(memory_space=pltpu.VMEM)
HBM = pl.BlockSpec(memory_space=pltpu.HBM)
SMEM = pl.BlockSpec(memory_space=pltpu.SMEM)
COPIES = 4
UNROLL = 4


def iota(shape, dim):
    return lax.broadcasted_iota(jnp.int32, shape, dim)


def pick(values, index):
    return jnp.take_along_axis(values, index, axis=1, mode="promise_in_bounds")


def swap_rows(x, even):
    return jnp.where(even, pltpu.roll(x, 7, 0), pltpu.roll(x, 1, 0))


def edges_kernel(moist, warm, old_moist, old_warm, blend, top, bottom, left, right, stage, arrived):
    planes, rows, cols = moist.shape
    parts = 2
    step = planes // parts
    copies = []
    for field, (now, old) in enumerate(((moist, old_moist), (warm, old_warm))):
        for part in range(parts):
            span = pl.ds(part * step, step)
            row = []
            for level, source in enumerate((now, old)):
                slot = (field * parts + part) * 2 + level
                row.append(
                    pltpu.make_async_copy(
                        source.at[span], stage.at[2 * field + level, span], arrived.at[slot]
                    )
                )
                row[-1].start()
            copies.append((field, part, row))
    for field, part, row in copies:
        for copy in row:
            copy.wait()
        for pair in range(part * step // 2, (part + 1) * step // 2):
            halves = []
            for plane in (2 * pair, 2 * pair + 1):
                mixed = 1.5 * stage[2 * field, plane] - 0.5 * stage[2 * field + 1, plane]
                blend[field, plane] = mixed
                top[field, plane] = mixed[0:2]
                bottom[field, plane] = mixed[rows - 2 : rows]
                halves.append(mixed)
            turned = jnp.concatenate(halves, axis=0).T
            at = (field * planes // 2 + pair) * 2 * rows
            left[:, pl.ds(at, 2 * rows)] = turned[0:2]
            right[:, pl.ds(at, 2 * rows)] = turned[cols - 2 : cols]


def gather_kernel(start, turn, tally, moist, warm, factors, surface, owner, scaled, fronts, sums, table):
    planes, rows, cols = moist.shape
    groups = surface.shape[0]
    drops = sums.shape[1]
    for plane in range(planes):
        below = (plane - 1) % planes
        table[pl.ds(plane * rows * 4, rows, stride=4), :] = moist[plane]
        table[pl.ds(plane * rows * 4 + 1, rows, stride=4), :] = warm[plane]
        table[pl.ds(below * rows * 4 + 2, rows, stride=4), :] = moist[plane]
        table[pl.ds(below * rows * 4 + 3, rows, stride=4), :] = warm[plane]
    live = tally[0, 0]
    lane = iota((8, LANES), 1)
    sub = iota((8, LANES), 0)
    even = (sub & 1) == 0
    even_lane = (lane & 1) == 0

    def raw(block):
        blocks = []
        for half in range(2 * UNROLL):
            found = jnp.zeros((8, LANES), jnp.float32)
            for j in range(HALF):
                at = block * (UNROLL * LANES) + half * HALF + j
                entry = pltpu.roll(table[pl.ds(start[at], 8), :], turn[at], 1)
                found = jnp.where(lane >= 2 * j, entry, found)
            blocks.append(found)
        return blocks

    def refine(block, blocks, total):
        terms = []
        tables = []
        for unit in range(UNROLL):
            group = block * UNROLL + unit
            corner = factors[pl.ds(group, 8, stride=groups), :]
            corner = jnp.where(
                (sub == 2) | (sub == 3),
                pltpu.roll(corner, 6, 0),
                jnp.where((sub == 4) | (sub == 5), pltpu.roll(corner, 2, 0), corner),
            )
            other = swap_rows(corner, even)
            area = jnp.broadcast_to(surface[pl.ds(group, 1), :], (8, LANES))
            area = jnp.where(lane + group * LANES < live, area, 0.0)
            values = []
            for half in range(2):
                spread = (lane >> 1) + half * HALF
                weight = jnp.where(even_lane == even, pick(corner, spread), pick(other, spread))
                value = blocks[2 * unit + half] * weight
                value = value + pltpu.roll(value, 2, 0)
                value = value + pltpu.roll(value, 4, 0)
                value = value + jnp.where(even_lane, pltpu.roll(value, 127, 1), pltpu.roll(value, 1, 1))
                at = pl.ds(pl.multiple_of((group * 2 + half) * 8, 8), 8)
                scaled[at, :] = weight * pick(area, spread)
                fronts[at, :] = jnp.where(even, value, value - 0.5 * pltpu.roll(value, 1, 0))
                values.append(pick(value, (lane * 2) & 127))
            value = jnp.where(lane < HALF, values[0], values[1])
            term = jnp.where(sub == 2, 1.0, value) * area
            high = term.astype(jnp.bfloat16).astype(jnp.float32)
            terms.append(jnp.concatenate([high, term - high], axis=0).astype(jnp.bfloat16))
            label = jnp.broadcast_to(owner[pl.ds(group, 1), :], (drops, LANES))
            tables.append((label == iota((drops, LANES), 0)).astype(jnp.float32).astype(jnp.bfloat16))
        return total + lax.dot_general(
            jnp.concatenate(terms, axis=1),
            jnp.concatenate(tables, axis=1),
            (((1,), (1,)), ((), ())),
            preferred_element_type=jnp.float32,
        )

    def step(block, carry):
        total, *blocks = carry
        later = raw(block)
        return (refine(block - 1, blocks, total), *later)

    count = groups // UNROLL
    carry = (jnp.zeros((16, drops), jnp.float32), *raw(0))
    total, *blocks = lax.fori_loop(1, count, step, carry)
    total = refine(count - 1, blocks, total)
    sums[...] = total[0:8] + total[8:16]


def stencil_kernel(blend, moist, warm, speed, above, below, left, right, out_moist, out_warm, padded, side):
    planes, rows, cols = moist.shape
    for field in range(2):
        for plane in range(planes):
            padded[field, plane, 8 : rows + 8, :] = blend[field, plane]
            padded[field, plane, 6:8, :] = above[field, plane]
            padded[field, plane, rows + 8 : rows + 10, :] = below[field, plane]
        for pair in range(planes // 2):
            slot = field * (planes // 2) + pair
            at = slot * 2 * rows
            block = jnp.concatenate(
                [
                    right[:, pl.ds(at, 2 * rows)],
                    jnp.zeros((cols - 4, 2 * rows), jnp.float32),
                    left[:, pl.ds(at, 2 * rows)],
                ],
                axis=0,
            )
            side[pl.ds(slot * 2 * rows, 2 * rows), :] = block.T
    lane = iota((rows, cols), 1)
    fraction = increment_span / 12.0

    def plane_step(plane, carry):
        speeds = [speed[k, plane].astype(jnp.float32) * fraction for k in range(3)]
        for field, (now, out) in enumerate(((moist, out_moist), (warm, out_warm))):
            center = padded[field, plane, 8 : rows + 8, :]
            edge = side[pl.ds(pl.multiple_of((field * planes + plane) * rows, rows), rows), :]
            wrap = lambda shift: padded[field, lax.rem(plane + shift + planes, planes), 8 : rows + 8, :]
            shift = lambda by: padded[field, plane, 8 + by : rows + 8 + by, :]
            around = [
                (wrap(1), wrap(2), wrap(-1), wrap(-2)),
                (shift(1), shift(2), shift(-1), shift(-2)),
                (
                    pltpu.roll(jnp.where(lane < 1, edge, center), cols - 1, 1),
                    pltpu.roll(jnp.where(lane < 2, edge, center), cols - 2, 1),
                    pltpu.roll(jnp.where(lane >= cols - 1, edge, center), 1, 1),
                    pltpu.roll(jnp.where(lane >= cols - 2, edge, center), 2, 1),
                ),
            ]
            near = 0.0
            far = 0.0
            total = now[plane] - (90.0 * diffusivity * fraction) * center
            for k, (ahead_one, ahead_two, behind_one, behind_two) in enumerate(around):
                near = near + (ahead_one + behind_one)
                far = far + (ahead_two + behind_two)
                total = total - speeds[k] * (8.0 * (ahead_one - behind_one) - (ahead_two - behind_two))
            out[plane] = total + (diffusivity * fraction) * (16.0 * near - far)
        return carry

    lax.fori_loop(0, planes, plane_step, 0)


def scatter_kernel(begin, turn, scaled, fronts, owner, sums, start_moist, start_warm, out_moist, out_warm, *banks):
    planes, rows, cols = start_moist.shape
    groups = owner.shape[0]
    drops = sums.shape[1]
    size = banks[0].shape[0]

    def clear(step, carry):
        for bank in banks:
            bank[pl.ds(pl.multiple_of(step * 128, 128), 128), :] = jnp.zeros((128, cols), jnp.float32)
        return carry

    lax.fori_loop(0, size // 128, clear, 0)
    totals = sums[...]
    drop_vapour = totals[0:1] / totals[2:3]
    drop_warmth = totals[1:2] / totals[2:3]
    saturated = 0.5 * jnp.exp(saturation_rate * (drop_warmth - 1.0))
    for_mass = 2.0 * saturated - drop_vapour
    for_heat = drop_warmth - 0.5 * for_mass
    wide = (8, drops)
    both = jnp.where(
        (iota(wide, 0) & 1) == 0, jnp.broadcast_to(for_mass, wide), jnp.broadcast_to(for_heat, wide)
    )
    pieces = []
    for at in range(0, drops, LANES):
        piece = both[:, at : min(at + LANES, drops)]
        if piece.shape[1] < LANES:
            piece = jnp.concatenate([piece, jnp.zeros((8, LANES - piece.shape[1]), jnp.float32)], axis=1)
        pieces.append(piece)

    lane = iota((8, LANES), 1)

    def ready(block):
        values = []
        for unit in range(UNROLL):
            group = block * UNROLL + unit
            label = jnp.broadcast_to(owner[pl.ds(group, 1), :], (8, LANES))
            looked = pick(pieces[0], label & 127)
            for number in range(1, len(pieces)):
                looked = jnp.where(label >= number * LANES, pick(pieces[number], label & 127), looked)
            for half in range(2):
                at = pl.ds(pl.multiple_of((group * 2 + half) * 8, 8), 8)
                values.append(scaled[at, :] * (pick(looked, (lane >> 1) + half * HALF) - fronts[at, :]))
        return values

    def spill(block, values):
        for half in range(2 * UNROLL):
            for j in range(HALF):
                at = block * (UNROLL * LANES) + half * HALF + j
                entry = jnp.where((lane >> 1) == j, values[half], 0.0)
                banks[j % len(banks)][pl.ds(begin[at], 8), :] += pltpu.roll(entry, turn[at], 1)

    def step(block, values):
        later = ready(block + 1)
        spill(block, values)
        return tuple(later)

    count = groups // UNROLL
    values = lax.fori_loop(0, count - 1, step, tuple(ready(0)))
    spill(count - 1, values)
    for plane in range(planes):
        before = (plane - 1) % planes
        for field, (start, out) in enumerate(((start_moist, out_moist), (start_warm, out_warm))):
            total = start[plane]
            for bank in banks:
                total = total + bank[pl.ds(plane * rows * 4 + field, rows, stride=4), :]
                total = total + bank[pl.ds(before * rows * 4 + 2 + field, rows, stride=4), :]
            out[plane] = total


def params(megabytes=40):
    return pltpu.CompilerParams(vmem_limit_bytes=megabytes << 20)


def shards(
    gas_moisture,
    gas_warmth,
    prior_moisture,
    prior_warmth,
    flow_speeds,
    lower_base_cell,
    trilinear_factors,
    panel_surface,
    panel_owner,
    active_panel_tally,
):
    planes, rows, cols = gas_moisture.shape
    drops = DROP_DEV * lax.axis_size("gx")
    count = panel_surface.shape[1]
    groups = count // LANES
    f32 = jnp.float32
    shape = jax.ShapeDtypeStruct
    row_local = lower_base_cell[1, 0] - lax.axis_index("gx") * rows
    col_local = lower_base_cell[2, 0] - lax.axis_index("gy") * cols
    turn = (2 * (jnp.arange(count, dtype=jnp.int32) % HALF) - col_local) & 127
    back = (128 - turn) & 127
    start = (lower_base_cell[0, 0] * rows + row_local) * 4
    factors = trilinear_factors.reshape(8 * groups, LANES)
    surface = panel_surface.reshape(groups, LANES)
    owner = panel_owner.reshape(groups, LANES)
    field = shape((planes, rows, cols), f32)

    blend, top, bottom, left, right = pl.pallas_call(
        edges_kernel,
        out_shape=(
            shape((2, planes, rows, cols), f32),
            shape((2, planes, 2, cols), f32),
            shape((2, planes, 2, cols), f32),
            shape((2, 2 * planes * rows), f32),
            shape((2, 2 * planes * rows), f32),
        ),
        in_specs=[HBM] * 4,
        out_specs=[VMEM] * 5,
        scratch_shapes=[pltpu.VMEM((4, planes, rows, cols), f32), pltpu.SemaphoreType.DMA((8,))],
        compiler_params=params(),
        name="edges",
    )(gas_moisture, gas_warmth, prior_moisture, prior_warmth)

    def around(axis, head, tail):
        size = lax.axis_size(axis)
        onward = [(i, (i + 1) % size) for i in range(size)]
        backward = [((i + 1) % size, i) for i in range(size)]
        return lax.ppermute(tail, axis, onward), lax.ppermute(head, axis, backward)

    above, below = around("gx", top, bottom)
    from_left, from_right = around("gy", left, right)

    scaled, fronts, sums = pl.pallas_call(
        gather_kernel,
        out_shape=(
            shape((2 * groups * 8, LANES), f32),
            shape((2 * groups * 8, LANES), f32),
            shape((8, drops), f32),
        ),
        in_specs=[SMEM] * 3 + [VMEM] * 5,
        out_specs=[VMEM] * 3,
        scratch_shapes=[pltpu.VMEM((planes * rows * 4 + 8, cols), f32)],
        compiler_params=params(),
        name="gather",
    )(start, turn, active_panel_tally, gas_moisture, gas_warmth, factors, surface, owner)

    totals = sums
    size = lax.axis_size("gx")
    if size & (size - 1):
        totals = lax.psum(totals, "gx")
    else:
        for bit in range(size.bit_length() - 1):
            swap = [(i, i ^ (1 << bit)) for i in range(size)]
            totals = totals + lax.ppermute(totals, "gx", swap)

    start_moist, start_warm = pl.pallas_call(
        stencil_kernel,
        out_shape=(field, field),
        in_specs=[VMEM] * 8,
        out_specs=[VMEM] * 2,
        scratch_shapes=[
            pltpu.VMEM((2, planes, rows + 16, cols), f32),
            pltpu.VMEM((2 * planes * rows, cols), f32),
        ],
        compiler_params=params(),
        name="stencil",
    )(blend, gas_moisture, gas_warmth, flow_speeds, above, below, from_left, from_right)

    size = planes * rows * 4 + 128
    return pl.pallas_call(
        scatter_kernel,
        out_shape=(field, field),
        in_specs=[SMEM] * 2 + [VMEM] * 6,
        out_specs=[VMEM] * 2,
        scratch_shapes=[pltpu.VMEM((size, cols), f32)] * COPIES,
        compiler_params=params(),
        name="scatter",
    )(start, back, scaled, fronts, owner, totals, start_moist, start_warm)


def solution(mesh):
    return jax.shard_map(
        shards,
        mesh=mesh,
        in_specs=(
            P(None, "gx", "gy"),
            P(None, "gx", "gy"),
            P(None, "gx", "gy"),
            P(None, "gx", "gy"),
            P(None, None, "gx", "gy"),
            P(None, "gy", "gx"),
            P(None, "gy", "gx"),
            P("gy", "gx"),
            P("gy", "gx"),
            P("gy", "gx"),
        ),
        out_specs=(P(None, "gx", "gy"), P(None, "gx", "gy")),
        check_vma=False,
    )
```

```python
import functools

import jax
import jax.numpy as jnp
from jax import lax
from jax.experimental import pallas as pl
from jax.experimental.pallas import tpu as pltpu
from jax.sharding import PartitionSpec as P

DROP_DEV = 20
LANES = 128
HALF = 64

increment_span = 0.1
diffusivity = 1.0
mass_rate = 2.0
saturation_rate = 2.0
thermal_flux = 1.0
enthalpy_evaporation = 0.5

VMEM = pl.BlockSpec(memory_space=pltpu.VMEM)
HBM = pl.BlockSpec(memory_space=pltpu.HBM)
SMEM = pl.BlockSpec(memory_space=pltpu.SMEM)
COPIES = 4
UNROLL = 4
EDGES = 62


def iota(shape, dim):
    return lax.broadcasted_iota(jnp.int32, shape, dim)


def pick(values, index):
    return jnp.take_along_axis(values, index, axis=1, mode="promise_in_bounds")


def swap_rows(x, even):
    return jnp.where(even, pltpu.roll(x, 7, 0), pltpu.roll(x, 1, 0))


def edges_kernel(moist, warm, old_moist, old_warm, top, bottom, left, right, stage, arrived):
    planes, rows, cols = moist.shape
    parts = 2
    step = planes // parts
    copies = []
    for field, (now, old) in enumerate(((moist, old_moist), (warm, old_warm))):
        for part in range(parts):
            span = pl.ds(part * step, step)
            row = []
            for level, source in enumerate((now, old)):
                slot = (field * parts + part) * 2 + level
                row.append(
                    pltpu.make_async_copy(
                        source.at[span], stage.at[2 * field + level, span], arrived.at[slot]
                    )
                )
                row[-1].start()
            copies.append((field, part, row))
    for field, part, row in copies:
        for copy in row:
            copy.wait()
        for pair in range(part * step // 2, (part + 1) * step // 2):
            halves = []
            for plane in (2 * pair, 2 * pair + 1):
                mixed = 1.5 * stage[2 * field, plane] - 0.5 * stage[2 * field + 1, plane]
                top[field, plane] = mixed[0:2]
                bottom[field, plane] = mixed[rows - 2 : rows]
                halves.append(mixed)
            turned = jnp.concatenate(halves, axis=0).T
            at = (field * planes // 2 + pair) * 2 * rows
            left[:, pl.ds(at, 2 * rows)] = turned[0:2]
            right[:, pl.ds(at, 2 * rows)] = turned[cols - 2 : cols]


def gather_kernel(start, turn, tally, moist, warm, factors, surface, owner, scaled, fronts, sums, table):
    planes, rows, cols = moist.shape
    groups = surface.shape[0]
    drops = sums.shape[1]
    for plane in range(planes):
        below = (plane - 1) % planes
        table[pl.ds(plane * rows * 4, rows, stride=4), :] = moist[plane]
        table[pl.ds(plane * rows * 4 + 1, rows, stride=4), :] = warm[plane]
        table[pl.ds(below * rows * 4 + 2, rows, stride=4), :] = moist[plane]
        table[pl.ds(below * rows * 4 + 3, rows, stride=4), :] = warm[plane]
    live = tally[0, 0]
    lane = iota((8, LANES), 1)
    sub = iota((8, LANES), 0)
    even = (sub & 1) == 0
    even_lane = (lane & 1) == 0

    def raw(block):
        blocks = []
        for half in range(2 * UNROLL):
            found = jnp.zeros((8, LANES), jnp.float32)
            for j in range(HALF):
                at = block * (UNROLL * LANES) + half * HALF + j
                entry = pltpu.roll(table[pl.ds(start[at], 8), :], turn[at], 1)
                found = jnp.where(lane >= 2 * j, entry, found)
            blocks.append(found)
        return blocks

    def refine(block, blocks, total):
        terms = []
        tables = []
        for unit in range(UNROLL):
            group = block * UNROLL + unit
            corner = factors[pl.ds(group, 8, stride=groups), :]
            corner = jnp.where(
                (sub == 2) | (sub == 3),
                pltpu.roll(corner, 6, 0),
                jnp.where((sub == 4) | (sub == 5), pltpu.roll(corner, 2, 0), corner),
            )
            other = swap_rows(corner, even)
            area = jnp.broadcast_to(surface[pl.ds(group, 1), :], (8, LANES))
            area = jnp.where(lane + group * LANES < live, area, 0.0)
            values = []
            for half in range(2):
                spread = (lane >> 1) + half * HALF
                weight = jnp.where(even_lane == even, pick(corner, spread), pick(other, spread))
                value = blocks[2 * unit + half] * weight
                value = value + pltpu.roll(value, 2, 0)
                value = value + pltpu.roll(value, 4, 0)
                value = value + jnp.where(even_lane, pltpu.roll(value, 127, 1), pltpu.roll(value, 1, 1))
                at = pl.ds(pl.multiple_of((group * 2 + half) * 8, 8), 8)
                scaled[at, :] = weight * pick(area, spread)
                fronts[at, :] = jnp.where(even, value, value - 0.5 * pltpu.roll(value, 1, 0))
                values.append(pick(value, (lane * 2) & 127))
            value = jnp.where(lane < HALF, values[0], values[1])
            term = jnp.where(sub == 2, 1.0, value) * area
            high = term.astype(jnp.bfloat16).astype(jnp.float32)
            terms.append(jnp.concatenate([high, term - high], axis=0).astype(jnp.bfloat16))
            label = jnp.broadcast_to(owner[pl.ds(group, 1), :], (drops, LANES))
            tables.append((label == iota((drops, LANES), 0)).astype(jnp.float32).astype(jnp.bfloat16))
        return total + lax.dot_general(
            jnp.concatenate(terms, axis=1),
            jnp.concatenate(tables, axis=1),
            (((1,), (1,)), ((), ())),
            preferred_element_type=jnp.float32,
        )

    def step(block, carry):
        total, *blocks = carry
        later = raw(block)
        return (refine(block - 1, blocks, total), *later)

    count = groups // UNROLL
    carry = (jnp.zeros((16, drops), jnp.float32), *raw(0))
    total, *blocks = lax.fori_loop(1, count, step, carry)
    total = refine(count - 1, blocks, total)
    sums[...] = total[0:8] + total[8:16]


def prepare(fields, halos, padded, side):
    above, below, left, right = halos
    planes, rows, cols = fields[0][0].shape
    for field, (now, old) in enumerate(fields):
        for plane in range(planes):
            padded[field, plane, 8 : rows + 8, :] = 1.5 * now[plane] - 0.5 * old[plane]
            padded[field, plane, 6:8, :] = above[field, plane]
            padded[field, plane, rows + 8 : rows + 10, :] = below[field, plane]
        for pair in range(planes // 2):
            at = (field * (planes // 2) + pair) * 2 * rows
            block = jnp.concatenate(
                [
                    right[:, pl.ds(at, 2 * rows)],
                    jnp.zeros((cols - 4, 2 * rows), jnp.float32),
                    left[:, pl.ds(at, 2 * rows)],
                ],
                axis=0,
            )
            side[pl.ds(at, 2 * rows), :] = block.T


def advance(plane, fields, speed, padded, side, outs):
    planes, rows, cols = fields[0][0].shape
    lane = iota((rows, cols), 1)
    fraction = increment_span / 12.0
    speeds = [speed[k, plane].astype(jnp.float32) * fraction for k in range(3)]
    for field in range(2):
        center = padded[field, plane, 8 : rows + 8, :]
        edge = side[pl.ds(pl.multiple_of((field * planes + plane) * rows, rows), rows), :]
        wrap = lambda shift: padded[field, lax.rem(plane + shift + planes, planes), 8 : rows + 8, :]
        shift = lambda by: padded[field, plane, 8 + by : rows + 8 + by, :]
        around = [
            (wrap(1), wrap(2), wrap(-1), wrap(-2)),
            (shift(1), shift(2), shift(-1), shift(-2)),
            (
                pltpu.roll(jnp.where(lane < 1, edge, center), cols - 1, 1),
                pltpu.roll(jnp.where(lane < 2, edge, center), cols - 2, 1),
                pltpu.roll(jnp.where(lane >= cols - 1, edge, center), 1, 1),
                pltpu.roll(jnp.where(lane >= cols - 2, edge, center), 2, 1),
            ),
        ]
        near = 0.0
        far = 0.0
        total = fields[field][0][plane] - (90.0 * diffusivity * fraction) * center
        for k, (ahead_one, ahead_two, behind_one, behind_two) in enumerate(around):
            near = near + (ahead_one + behind_one)
            far = far + (ahead_two + behind_two)
            total = total - speeds[k] * (8.0 * (ahead_one - behind_one) - (ahead_two - behind_two))
        outs[field][plane] = total + (diffusivity * fraction) * (16.0 * near - far)


def scatter_kernel(
    begin,
    turn,
    scaled,
    fronts,
    owner,
    sums,
    moist,
    warm,
    old_moist,
    old_warm,
    speed,
    above,
    below,
    left,
    right,
    out_moist,
    out_warm,
    padded,
    side,
    *banks,
):
    planes, rows, cols = moist.shape
    groups = owner.shape[0]
    drops = sums.shape[1]
    size = banks[0].shape[0]
    fields = ((moist, old_moist), (warm, old_warm))
    outs = (out_moist, out_warm)
    prepare(fields, (above, below, left, right), padded, side)

    def clear(step, carry):
        for bank in banks:
            bank[pl.ds(pl.multiple_of(step * 128, 128), 128), :] = jnp.zeros((128, cols), jnp.float32)
        return carry

    lax.fori_loop(0, size // 128, clear, 0)
    totals = sums[...]
    drop_vapour = totals[0:1] / totals[2:3]
    drop_warmth = totals[1:2] / totals[2:3]
    saturated = 0.5 * jnp.exp(saturation_rate * (drop_warmth - 1.0))
    for_mass = 2.0 * saturated - drop_vapour
    for_heat = drop_warmth - 0.5 * for_mass
    wide = (8, drops)
    both = jnp.where(
        (iota(wide, 0) & 1) == 0, jnp.broadcast_to(for_mass, wide), jnp.broadcast_to(for_heat, wide)
    )
    pieces = []
    for at in range(0, drops, LANES):
        piece = both[:, at : min(at + LANES, drops)]
        if piece.shape[1] < LANES:
            piece = jnp.concatenate([piece, jnp.zeros((8, LANES - piece.shape[1]), jnp.float32)], axis=1)
        pieces.append(piece)

    lane = iota((8, LANES), 1)

    def ready(block):
        values = []
        for unit in range(UNROLL):
            group = block * UNROLL + unit
            label = jnp.broadcast_to(owner[pl.ds(group, 1), :], (8, LANES))
            looked = pick(pieces[0], label & 127)
            for number in range(1, len(pieces)):
                looked = jnp.where(label >= number * LANES, pick(pieces[number], label & 127), looked)
            for half in range(2):
                at = pl.ds(pl.multiple_of((group * 2 + half) * 8, 8), 8)
                values.append(scaled[at, :] * (pick(looked, (lane >> 1) + half * HALF) - fronts[at, :]))
        return values

    def spill(block, values):
        for half in range(2 * UNROLL):
            for j in range(HALF):
                at = block * (UNROLL * LANES) + half * HALF + j
                entry = jnp.where((lane >> 1) == j, values[half], 0.0)
                banks[j % len(banks)][pl.ds(begin[at], 8), :] += pltpu.roll(entry, turn[at], 1)

    def grid_share(block):
        for number in range(planes // count):
            advance(block * (planes // count) + number, fields, speed, padded, side, outs)

    def step(block, values):
        later = ready(block + 1)
        grid_share(block)
        spill(block, values)
        return tuple(later)

    count = groups // UNROLL
    values = lax.fori_loop(0, count - 1, step, tuple(ready(0)))
    grid_share(count - 1)
    spill(count - 1, values)
    for plane in range(planes):
        before = (plane - 1) % planes
        for field, out in enumerate(outs):
            total = out[plane]
            for bank in banks:
                total = total + bank[pl.ds(plane * rows * 4 + field, rows, stride=4), :]
                total = total + bank[pl.ds(before * rows * 4 + 2 + field, rows, stride=4), :]
            out[plane] = total


def params(megabytes=40):
    return pltpu.CompilerParams(vmem_limit_bytes=megabytes << 20)


def shards(
    gas_moisture,
    gas_warmth,
    prior_moisture,
    prior_warmth,
    flow_speeds,
    lower_base_cell,
    trilinear_factors,
    panel_surface,
    panel_owner,
    active_panel_tally,
):
    planes, rows, cols = gas_moisture.shape
    drops = DROP_DEV * lax.axis_size("gx")
    count = panel_surface.shape[1]
    groups = count // LANES
    f32 = jnp.float32
    shape = jax.ShapeDtypeStruct
    row_local = lower_base_cell[1, 0] - lax.axis_index("gx") * rows
    col_local = lower_base_cell[2, 0] - lax.axis_index("gy") * cols
    turn = (2 * (jnp.arange(count, dtype=jnp.int32) % HALF) - col_local) & 127
    back = (128 - turn) & 127
    start = (lower_base_cell[0, 0] * rows + row_local) * 4
    factors = trilinear_factors.reshape(8 * groups, LANES)
    surface = panel_surface.reshape(groups, LANES)
    owner = panel_owner.reshape(groups, LANES)
    field = shape((planes, rows, cols), f32)

    top, bottom, left, right = pl.pallas_call(
        edges_kernel,
        out_shape=(
            shape((2, planes, 2, cols), f32),
            shape((2, planes, 2, cols), f32),
            shape((2, 2 * planes * rows), f32),
            shape((2, 2 * planes * rows), f32),
        ),
        in_specs=[HBM] * 4,
        out_specs=[VMEM] * 4,
        scratch_shapes=[pltpu.VMEM((4, planes, rows, cols), f32), pltpu.SemaphoreType.DMA((8,))],
        compiler_params=params(EDGES),
        name="edges",
    )(gas_moisture, gas_warmth, prior_moisture, prior_warmth)

    def around(axis, head, tail):
        size = lax.axis_size(axis)
        onward = [(i, (i + 1) % size) for i in range(size)]
        backward = [((i + 1) % size, i) for i in range(size)]
        return lax.ppermute(tail, axis, onward), lax.ppermute(head, axis, backward)

    above, below = around("gx", top, bottom)
    from_left, from_right = around("gy", left, right)

    scaled, fronts, sums = pl.pallas_call(
        gather_kernel,
        out_shape=(
            shape((2 * groups * 8, LANES), f32),
            shape((2 * groups * 8, LANES), f32),
            shape((8, drops), f32),
        ),
        in_specs=[SMEM] * 3 + [VMEM] * 5,
        out_specs=[VMEM] * 3,
        scratch_shapes=[pltpu.VMEM((planes * rows * 4 + 8, cols), f32)],
        compiler_params=params(),
        name="gather",
    )(start, turn, active_panel_tally, gas_moisture, gas_warmth, factors, surface, owner)

    totals = sums
    size = lax.axis_size("gx")
    if size & (size - 1):
        totals = lax.psum(totals, "gx")
    else:
        for bit in range(size.bit_length() - 1):
            swap = [(i, i ^ (1 << bit)) for i in range(size)]
            totals = totals + lax.ppermute(totals, "gx", swap)

    size = planes * rows * 4 + 128
    return pl.pallas_call(
        scatter_kernel,
        out_shape=(field, field),
        in_specs=[SMEM] * 2 + [VMEM] * 13,
        out_specs=[VMEM] * 2,
        scratch_shapes=[
            pltpu.VMEM((2, planes, rows + 16, cols), f32),
            pltpu.VMEM((2 * planes * rows, cols), f32),
        ]
        + [pltpu.VMEM((size, cols), f32)] * COPIES,
        compiler_params=params(),
        name="scatter",
    )(
        start,
        back,
        scaled,
        fronts,
        owner,
        totals,
        gas_moisture,
        gas_warmth,
        prior_moisture,
        prior_warmth,
        flow_speeds,
        above,
        below,
        from_left,
        from_right,
    )


def solution(mesh):
    return jax.shard_map(
        shards,
        mesh=mesh,
        in_specs=(
            P(None, "gx", "gy"),
            P(None, "gx", "gy"),
            P(None, "gx", "gy"),
            P(None, "gx", "gy"),
            P(None, None, "gx", "gy"),
            P(None, "gy", "gx"),
            P(None, "gy", "gx"),
            P("gy", "gx"),
            P("gy", "gx"),
            P("gy", "gx"),
        ),
        out_specs=(P(None, "gx", "gy"), P(None, "gx", "gy")),
        check_vma=False,
    )
```

```python
import functools

import jax
import jax.numpy as jnp
from jax import lax
from jax.experimental import pallas as pl
from jax.experimental.pallas import tpu as pltpu
from jax.sharding import PartitionSpec as P

DROP_DEV = 20
LANES = 128
HALF = 64

increment_span = 0.1
diffusivity = 1.0
mass_rate = 2.0
saturation_rate = 2.0
thermal_flux = 1.0
enthalpy_evaporation = 0.5

VMEM = pl.BlockSpec(memory_space=pltpu.VMEM)
HBM = pl.BlockSpec(memory_space=pltpu.HBM)
SMEM = pl.BlockSpec(memory_space=pltpu.SMEM)
COPIES = 4
UNROLL = 4
GATHER_MB = 53.85
SCATTER_MB = 53.65
PARTS = 4


def iota(shape, dim):
    return lax.broadcasted_iota(jnp.int32, shape, dim)


def pick(values, index):
    return jnp.take_along_axis(values, index, axis=1, mode="promise_in_bounds")


def swap_rows(x, even):
    return jnp.where(even, pltpu.roll(x, 7, 0), pltpu.roll(x, 1, 0))


def odd_row():
    return (lax.axis_index("gx") & 1) == 1


def fetch(source, target, arrived, slots):
    copy = pltpu.make_async_copy(source, target, arrived.at[slots.pop()])
    copy.start()
    return copy


def gather_kernel(
    base_in,
    tally_in,
    moist,
    warm,
    old_moist,
    old_warm,
    factors_in,
    surface_in,
    owner_in,
    start_out,
    back_out,
    owner_out,
    scaled_out,
    fronts_out,
    sums,
    facing,
    backing,
    head,
    tail,
    base,
    tally,
    factors,
    surface,
    owner,
    table,
    stage,
    scaled,
    fronts,
    places,
    start,
    turn,
    arrived,
):
    planes, rows, cols = moist.shape
    groups = surface.shape[0]
    count = groups // UNROLL
    head_rows = facing.shape[0] - backing.shape[0]
    step_planes = planes // PARTS
    slots = list(range(arrived.shape[0]))
    first = fetch(base_in, base, arrived, slots)
    copies = []
    for levels in ((0, 2), (1, 3)):
        for part in range(PARTS):
            for level in levels:
                span = pl.ds(part * step_planes, step_planes)
                source = (moist, old_moist, warm, old_warm)[level]
                copies.append(fetch(source.at[span], stage.at[level, span], arrived, slots))
    small = [
        fetch(source, target, arrived, slots)
        for source, target in (
            (factors_in, factors),
            (surface_in, surface),
            (owner_in, owner),
            (tally_in, tally),
        )
    ]
    first.wait()
    spot = (groups, LANES)
    column = base[2 * groups : 3 * groups, :] - lax.axis_index("gy") * cols
    twist = (2 * (iota(spot, 1) & (HALF - 1)) - column) & 127
    row = base[groups : 2 * groups, :] - lax.axis_index("gx") * rows
    places[0] = (base[0:groups, :] * rows + row) * 4
    places[1] = twist
    places[2] = (128 - twist) & 127
    indices = [fetch(places.at[0], start, arrived, slots), fetch(places.at[1], turn, arrived, slots)]
    results = [
        fetch(places.at[0], start_out, arrived, slots),
        fetch(places.at[2], back_out, arrived, slots),
    ]
    facing[0:head_rows, :] = jnp.zeros((head_rows, LANES), jnp.float32)
    sums[...] = jnp.zeros(sums.shape, jnp.float32)
    for plane in range(planes):
        if plane % step_planes == 0:
            copies[plane // step_planes * 2].wait()
            copies[plane // step_planes * 2 + 1].wait()
        below = (plane - 1) % planes
        table[pl.ds(plane * rows * 4, rows, stride=4), :] = stage[0, plane]
        table[pl.ds(plane * rows * 4 + 1, rows, stride=4), :] = stage[2, plane]
        table[pl.ds(below * rows * 4 + 2, rows, stride=4), :] = stage[0, plane]
        table[pl.ds(below * rows * 4 + 3, rows, stride=4), :] = stage[2, plane]
    for copy in copies[2 * PARTS :] + indices + small:
        copy.wait()
    results.append(fetch(owner, owner_out, arrived, slots))
    odd = odd_row()
    drops = DROP_DEV * lax.axis_size("gx")

    def edges(block):
        share = planes // 2 // count
        for number in range(share):
            for field in range(2):
                pair = block * share + number
                halves = []
                for half in range(2):
                    plane = pair * 2 + half
                    mixed = 1.5 * stage[2 * field, plane] - 0.5 * stage[2 * field + 1, plane]
                    top, bottom = mixed[0:2], mixed[rows - 2 : rows]
                    at = (field * planes + plane) * 2
                    facing[pl.ds(head_rows + at, 2), :] = jnp.where(odd, top, bottom)
                    backing[pl.ds(at, 2), :] = jnp.where(odd, bottom, top)
                    halves.append(mixed)
                turned = jnp.concatenate(halves, axis=0).T
                at = pl.multiple_of((field * (planes // 2) + pair) * 2 * rows, 2 * rows)
                head[:, pl.ds(at, 2 * rows)] = turned[0:2]
                tail[:, pl.ds(at, 2 * rows)] = turned[cols - 2 : cols]

    lane = iota((8, LANES), 1)
    live = jnp.broadcast_to(tally[...], (8, LANES))
    sub = iota((8, LANES), 0)
    even = (sub & 1) == 0
    even_lane = (lane & 1) == 0

    def raw(block):
        blocks = []
        for half in range(2 * UNROLL):
            found = jnp.zeros((8, LANES), jnp.float32)
            for j in range(HALF):
                at = (block * UNROLL + half // 2, half % 2 * HALF + j)
                entry = pltpu.roll(table[pl.ds(start[at], 8), :], turn[at], 1)
                found = jnp.where(lane >= 2 * j, entry, found)
            blocks.append(found)
        return blocks

    def refine(block, blocks, total):
        terms = []
        tables = []
        for unit in range(UNROLL):
            group = block * UNROLL + unit
            corner = factors[pl.ds(group, 8, stride=groups), :]
            corner = jnp.where(
                (sub == 2) | (sub == 3),
                pltpu.roll(corner, 6, 0),
                jnp.where((sub == 4) | (sub == 5), pltpu.roll(corner, 2, 0), corner),
            )
            other = swap_rows(corner, even)
            area = jnp.broadcast_to(surface[pl.ds(group, 1), :], (8, LANES))
            area = jnp.where(lane + group * LANES < live, area, 0.0)
            values = []
            for half in range(2):
                spread = (lane >> 1) + half * HALF
                weight = jnp.where(even_lane == even, pick(corner, spread), pick(other, spread))
                value = blocks[2 * unit + half] * weight
                value = value + pltpu.roll(value, 2, 0)
                value = value + pltpu.roll(value, 4, 0)
                value = value + jnp.where(even_lane, pltpu.roll(value, 127, 1), pltpu.roll(value, 1, 1))
                at = pl.ds(pl.multiple_of((group * 2 + half) * 8, 8), 8)
                scaled[at, :] = weight * pick(area, spread)
                fronts[at, :] = jnp.where(even, value, value - 0.5 * pltpu.roll(value, 1, 0))
                values.append(pick(value, (lane * 2) & 127))
            value = jnp.where(lane < HALF, values[0], values[1])
            term = jnp.where(sub == 2, 1.0, value) * area
            high = term.astype(jnp.bfloat16).astype(jnp.float32)
            terms.append(jnp.concatenate([high, term - high], axis=0).astype(jnp.bfloat16))
            label = jnp.broadcast_to(owner[pl.ds(group, 1), :], (drops, LANES))
            tables.append((label == iota((drops, LANES), 0)).astype(jnp.float32).astype(jnp.bfloat16))
        return total + lax.dot_general(
            jnp.concatenate(terms, axis=1),
            jnp.concatenate(tables, axis=1),
            (((1,), (1,)), ((), ())),
            preferred_element_type=jnp.float32,
        )

    tray = UNROLL * 16
    outward = [arrived.at[slots.pop()] for number in range(2)]

    def sends(block):
        span = pl.ds(pl.multiple_of(block * tray, tray), tray)
        return [
            pltpu.make_async_copy(scaled.at[span], scaled_out.at[span], outward[0]),
            pltpu.make_async_copy(fronts.at[span], fronts_out.at[span], outward[1]),
        ]

    def send(block):
        for copy in sends(block):
            copy.start()

    def step(block, carry):
        total, *blocks = carry
        later = raw(block)
        edges(block - 1)
        total = refine(block - 1, blocks, total)
        send(block - 1)
        return (total, *later)

    carry = (jnp.zeros((16, drops), jnp.float32), *raw(0))
    total, *blocks = lax.fori_loop(1, count, step, carry)
    edges(count - 1)
    total = refine(count - 1, blocks, total)
    send(count - 1)
    total = total[0:8] + total[8:16]
    for number, at in enumerate(range(0, drops, LANES)):
        size = min(LANES, drops - at)
        facing[8 * number : 8 * number + 8, 0:size] = total[:, at : at + size]
        sums[8 * number : 8 * number + 8, 0:size] = total[:, at : at + size]
    for copy in results:
        copy.wait()
    pltpu.make_async_copy(scaled, scaled_out, outward[0]).wait()
    pltpu.make_async_copy(fronts, fronts_out, outward[1]).wait()


def prepare(fields, halos, padded, side):
    facing, backing, left, right = halos
    planes, rows, cols = fields[0][0].shape
    head_rows = facing.shape[0] - backing.shape[0]
    odd = odd_row()
    for field, (now, old) in enumerate(fields):
        for plane in range(planes):
            padded[field, plane, 8 : rows + 8, :] = 1.5 * now[plane] - 0.5 * old[plane]
            at = (field * planes + plane) * 2
            near = facing[head_rows + at : head_rows + at + 2, :]
            far = backing[at : at + 2, :]
            padded[field, plane, 6:8, :] = jnp.where(odd, near, far)
            padded[field, plane, rows + 8 : rows + 10, :] = jnp.where(odd, far, near)
        for pair in range(planes // 2):
            at = (field * (planes // 2) + pair) * 2 * rows
            block = jnp.concatenate(
                [
                    right[:, pl.ds(at, 2 * rows)],
                    jnp.zeros((cols - 4, 2 * rows), jnp.float32),
                    left[:, pl.ds(at, 2 * rows)],
                ],
                axis=0,
            )
            side[pl.ds(at, 2 * rows), :] = block.T


def advance(plane, fields, speed, padded, side, outs):
    planes, rows, cols = fields[0][0].shape
    lane = iota((rows, cols), 1)
    fraction = increment_span / 12.0
    speeds = [speed[k, plane].astype(jnp.float32) * fraction for k in range(3)]
    for field in range(2):
        center = padded[field, plane, 8 : rows + 8, :]
        edge = side[pl.ds(pl.multiple_of((field * planes + plane) * rows, rows), rows), :]
        wrap = lambda shift: padded[field, lax.rem(plane + shift + planes, planes), 8 : rows + 8, :]
        shift = lambda by: padded[field, plane, 8 + by : rows + 8 + by, :]
        around = [
            (wrap(1), wrap(2), wrap(-1), wrap(-2)),
            (shift(1), shift(2), shift(-1), shift(-2)),
            (
                pltpu.roll(jnp.where(lane < 1, edge, center), cols - 1, 1),
                pltpu.roll(jnp.where(lane < 2, edge, center), cols - 2, 1),
                pltpu.roll(jnp.where(lane >= cols - 1, edge, center), 1, 1),
                pltpu.roll(jnp.where(lane >= cols - 2, edge, center), 2, 1),
            ),
        ]
        near = 0.0
        far = 0.0
        total = fields[field][0][plane] - (90.0 * diffusivity * fraction) * center
        for k, (ahead_one, ahead_two, behind_one, behind_two) in enumerate(around):
            near = near + (ahead_one + behind_one)
            far = far + (ahead_two + behind_two)
            total = total - speeds[k] * (8.0 * (ahead_one - behind_one) - (ahead_two - behind_two))
        outs[field][plane] = total + (diffusivity * fraction) * (16.0 * near - far)


def scatter_kernel(
    start_in,
    back_in,
    scaled_in,
    fronts_in,
    owner,
    sums,
    moist,
    warm,
    old_moist,
    old_warm,
    speed_in,
    facing,
    backing,
    left,
    right,
    out_moist,
    out_warm,
    padded,
    side,
    stage,
    speed,
    scaled,
    fronts,
    result,
    begin,
    turn,
    arrived,
    *banks,
):
    planes, rows, cols = moist.shape
    groups = owner.shape[0]
    size = banks[0].shape[0]
    step_planes = planes // PARTS
    slots = list(range(arrived.shape[0]))
    indices = [fetch(start_in, begin, arrived, slots), fetch(back_in, turn, arrived, slots)]
    copies = []
    for level, source in enumerate((moist, old_moist, warm, old_warm)):
        for part in range(PARTS):
            span = pl.ds(part * step_planes, step_planes)
            copies.append(fetch(source.at[span], stage.at[level, span], arrived, slots))
    copies.append(fetch(scaled_in, scaled, arrived, slots))
    copies.append(fetch(fronts_in, fronts, arrived, slots))
    copies += [fetch(speed_in.at[k], speed.at[k], arrived, slots) for k in range(3)]
    fields = ((stage.at[0], stage.at[1]), (stage.at[2], stage.at[3]))
    outs = (result.at[0], result.at[1])

    def clear(step, carry):
        for bank in banks:
            bank[pl.ds(pl.multiple_of(step * 128, 128), 128), :] = jnp.zeros((128, cols), jnp.float32)
        return carry

    lax.fori_loop(0, size // 128, clear, 0)
    pieces = []
    for at in range(0, sums.shape[0], 8):
        totals = sums[at : at + 8, :]
        drop_vapour = totals[0:1] / totals[2:3]
        drop_warmth = totals[1:2] / totals[2:3]
        saturated = 0.5 * jnp.exp(saturation_rate * (drop_warmth - 1.0))
        for_mass = 2.0 * saturated - drop_vapour
        for_heat = drop_warmth - 0.5 * for_mass
        wide = (8, LANES)
        pieces.append(
            jnp.where(
                (iota(wide, 0) & 1) == 0,
                jnp.broadcast_to(for_mass, wide),
                jnp.broadcast_to(for_heat, wide),
            )
        )
    for copy in indices + copies:
        copy.wait()
    prepare(fields, (facing, backing, left, right), padded, side)
    lane = iota((8, LANES), 1)

    def ready(block):
        values = []
        for unit in range(UNROLL):
            group = block * UNROLL + unit
            label = jnp.broadcast_to(owner[pl.ds(group, 1), :], (8, LANES))
            looked = pick(pieces[0], label & 127)
            for number in range(1, len(pieces)):
                looked = jnp.where(label >= number * LANES, pick(pieces[number], label & 127), looked)
            for half in range(2):
                at = pl.ds(pl.multiple_of((group * 2 + half) * 8, 8), 8)
                values.append(scaled[at, :] * (pick(looked, (lane >> 1) + half * HALF) - fronts[at, :]))
        return values

    def spill(block, values):
        for half in range(2 * UNROLL):
            for j in range(HALF):
                at = (block * UNROLL + half // 2, half % 2 * HALF + j)
                entry = jnp.where((lane >> 1) == j, values[half], 0.0)
                banks[j % len(banks)][pl.ds(begin[at], 8), :] += pltpu.roll(entry, turn[at], 1)

    def grid_share(block):
        for number in range(planes // count):
            advance(block * (planes // count) + number, fields, speed, padded, side, outs)

    def step(block, values):
        later = ready(block + 1)
        grid_share(block)
        spill(block, values)
        return tuple(later)

    count = groups // UNROLL
    values = lax.fori_loop(0, count - 1, step, tuple(ready(0)))
    grid_share(count - 1)
    spill(count - 1, values)
    finished = []
    for plane in range(planes):
        before = (plane - 1) % planes
        for field, out in enumerate(outs):
            total = out[plane]
            for bank in banks:
                total = total + bank[pl.ds(plane * rows * 4 + field, rows, stride=4), :]
                total = total + bank[pl.ds(before * rows * 4 + 2 + field, rows, stride=4), :]
            out[plane] = total
        if (plane + 1) % step_planes == 0:
            span = pl.ds(plane + 1 - step_planes, step_planes)
            for out, target in zip(outs, (out_moist, out_warm)):
                finished.append(fetch(out.at[span], target.at[span], arrived, slots))
    for copy in finished:
        copy.wait()


def params(megabytes=40):
    return pltpu.CompilerParams(vmem_limit_bytes=int(megabytes * 1024) << 10)


def shards(
    gas_moisture,
    gas_warmth,
    prior_moisture,
    prior_warmth,
    flow_speeds,
    lower_base_cell,
    trilinear_factors,
    panel_surface,
    panel_owner,
    active_panel_tally,
):
    planes, rows, cols = gas_moisture.shape
    drops = DROP_DEV * lax.axis_size("gx")
    count = panel_surface.shape[1]
    groups = count // LANES
    f32 = jnp.float32
    shape = jax.ShapeDtypeStruct
    base = lower_base_cell.reshape(3 * groups, LANES)
    factors = trilinear_factors.reshape(8 * groups, LANES)
    surface = panel_surface.reshape(groups, LANES)
    owner = panel_owner.reshape(groups, LANES)
    field = shape((planes, rows, cols), f32)

    head_rows = -(-drops // LANES) * 8
    edge_rows = 2 * planes * 2
    spots = shape((groups, LANES), jnp.int32)
    trays = shape((2 * groups * 8, LANES), f32)
    start, back, label, scaled, fronts, sums, facing, backing, head, tail = pl.pallas_call(
        gather_kernel,
        out_shape=(
            spots,
            spots,
            spots,
            trays,
            trays,
            shape((head_rows, cols), f32),
            shape((head_rows + edge_rows, cols), f32),
            shape((edge_rows, cols), f32),
            shape((2, 2 * planes * rows), f32),
            shape((2, 2 * planes * rows), f32),
        ),
        in_specs=[HBM] * 9,
        out_specs=[HBM] * 5 + [VMEM] * 5,
        scratch_shapes=[
            pltpu.VMEM(base.shape, jnp.int32),
            pltpu.VMEM((1, 1), jnp.int32),
            pltpu.VMEM(factors.shape, f32),
            pltpu.VMEM(surface.shape, f32),
            pltpu.VMEM(owner.shape, jnp.int32),
            pltpu.VMEM((planes * rows * 4 + 8, cols), f32),
            pltpu.VMEM((4, planes, rows, cols), f32),
            pltpu.VMEM(trays.shape, f32),
            pltpu.VMEM(trays.shape, f32),
            pltpu.VMEM((3, groups, LANES), jnp.int32),
            pltpu.SMEM((groups, LANES), jnp.int32),
            pltpu.SMEM((groups, LANES), jnp.int32),
            pltpu.SemaphoreType.DMA((4 * PARTS + 12,)),
        ],
        compiler_params=params(GATHER_MB),
        name="gather",
    )(
        base,
        active_panel_tally,
        gas_moisture,
        gas_warmth,
        prior_moisture,
        prior_warmth,
        factors,
        surface,
        owner,
    )

    def permute(x, axis, target):
        size = lax.axis_size(axis)
        return lax.ppermute(x, axis, [(i, target(i, size)) for i in range(size)])

    got_facing = permute(facing, "gx", lambda i, n: i ^ 1)
    got_backing = permute(backing, "gx", lambda i, n: (i - 1 if i % 2 == 0 else i + 1) % n)
    from_left = permute(tail, "gy", lambda i, n: (i + 1) % n)
    from_right = permute(head, "gy", lambda i, n: (i - 1) % n)
    totals = sums + got_facing[0:head_rows]
    size = lax.axis_size("gx")
    stride = 2
    while stride < size:
        if size % (2 * stride) == 0:
            totals = totals + permute(totals, "gx", lambda i, n: i ^ stride)
            stride *= 2
        else:
            partial = totals
            for number in range(1, size // stride):
                totals = totals + permute(
                    partial, "gx", lambda i, n: (i + number * stride) % n
                )
            stride = size

    size = planes * rows * 4 + 128
    return pl.pallas_call(
        scatter_kernel,
        out_shape=(field, field),
        in_specs=[HBM] * 4 + [VMEM] * 2 + [HBM] * 5 + [VMEM] * 4,
        out_specs=[HBM] * 2,
        scratch_shapes=[
            pltpu.VMEM((2, planes, rows + 16, cols), f32),
            pltpu.VMEM((2 * planes * rows, cols), f32),
            pltpu.VMEM((4, planes, rows, cols), f32),
            pltpu.VMEM((3, planes, rows, cols), jnp.bfloat16),
            pltpu.VMEM(trays.shape, f32),
            pltpu.VMEM(trays.shape, f32),
            pltpu.VMEM((2, planes, rows, cols), f32),
            pltpu.SMEM((groups, LANES), jnp.int32),
            pltpu.SMEM((groups, LANES), jnp.int32),
            pltpu.SemaphoreType.DMA((6 * PARTS + 7,)),
        ]
        + [pltpu.VMEM((size, cols), f32)] * COPIES,
        compiler_params=params(SCATTER_MB),
        name="scatter",
    )(
        start,
        back,
        scaled,
        fronts,
        label,
        totals,
        gas_moisture,
        gas_warmth,
        prior_moisture,
        prior_warmth,
        flow_speeds,
        got_facing,
        got_backing,
        from_left,
        from_right,
    )


def solution(mesh):
    return jax.shard_map(
        shards,
        mesh=mesh,
        in_specs=(
            P(None, "gx", "gy"),
            P(None, "gx", "gy"),
            P(None, "gx", "gy"),
            P(None, "gx", "gy"),
            P(None, None, "gx", "gy"),
            P(None, "gy", "gx"),
            P(None, "gy", "gx"),
            P("gy", "gx"),
            P("gy", "gx"),
            P("gy", "gx"),
        ),
        out_specs=(P(None, "gx", "gy"), P(None, "gx", "gy")),
        check_vma=False,
    )
```

```python
import functools

import jax
import jax.numpy as jnp
from jax import lax
from jax.experimental import pallas as pl
from jax.experimental.pallas import tpu as pltpu
from jax.sharding import PartitionSpec as P

DROP_DEV = 20
LANES = 128
HALF = 64

increment_span = 0.1
diffusivity = 1.0
mass_rate = 2.0
saturation_rate = 2.0
thermal_flux = 1.0
enthalpy_evaporation = 0.5

VMEM = pl.BlockSpec(memory_space=pltpu.VMEM)
HBM = pl.BlockSpec(memory_space=pltpu.HBM)
SMEM = pl.BlockSpec(memory_space=pltpu.SMEM)
COPIES = 4
UNROLL = 4
GATHER_MB = 16
SCATTER_MB = 20
PARTS = 4


def iota(shape, dim):
    return lax.broadcasted_iota(jnp.int32, shape, dim)


def pick(values, index):
    return jnp.take_along_axis(values, index, axis=1, mode="promise_in_bounds")


def swap_rows(x, even):
    return jnp.where(even, pltpu.roll(x, 7, 0), pltpu.roll(x, 1, 0))


def odd_row():
    return (lax.axis_index("gx") & 1) == 1


def fetch(source, target, arrived, slots):
    copy = pltpu.make_async_copy(source, target, arrived.at[slots.pop()])
    copy.start()
    return copy


def gather_kernel(
    tally,
    base_in,
    moist,
    warm,
    old_moist,
    old_warm,
    factors_in,
    surface_in,
    owner_in,
    speed_in,
    start_out,
    back_out,
    owner,
    scaled,
    fronts,
    now,
    padded,
    speed,
    sums,
    facing,
    backing,
    head,
    tail,
    base,
    factors,
    surface,
    table,
    old,
    columns,
    start,
    arrived,
):
    planes, rows, cols = moist.shape
    groups = surface.shape[0]
    count = groups // UNROLL
    head_rows = facing.shape[0] - backing.shape[0]
    step_planes = planes // PARTS
    slots = list(range(arrived.shape[0]))
    first = fetch(base_in, base, arrived, slots)
    copies = []
    for levels in ((0, 2), (1, 3)):
        for part in range(PARTS):
            for level in levels:
                span = pl.ds(part * step_planes, step_planes)
                source = (moist, old_moist, warm, old_warm)[level]
                target = (now, old)[level % 2].at[level // 2, span]
                copies.append(fetch(source.at[span], target, arrived, slots))
    small = [
        fetch(source, target, arrived, slots)
        for source, target in (
            (factors_in, factors),
            (surface_in, surface),
            (owner_in, owner),
        )
    ]
    later = [fetch(speed_in.at[k], speed.at[k], arrived, slots) for k in range(3)]
    first.wait()
    spot = (groups, LANES)
    column = base[2 * groups : 3 * groups, :] - lax.axis_index("gy") * cols
    row = base[groups : 2 * groups, :] - lax.axis_index("gx") * rows
    lane = iota((8, LANES), 1)
    for group in range(groups):
        wide = jnp.broadcast_to(column[group : group + 1], (8, LANES))
        for half in range(2):
            columns[(2 * group + half) * 8 : (2 * group + half) * 8 + 8, :] = (
                pick(wide, (lane >> 1) + half * HALF) + (lane & 1)
            )
    back_out[...] = (column - 2 * (iota(spot, 1) & (HALF - 1))) & 127
    start_out[...] = (base[0:groups, :] * rows + row) * 4
    indices = [fetch(start_out, start, arrived, slots)]
    facing[0:head_rows, :] = jnp.zeros((head_rows, LANES), jnp.float32)
    sums[...] = jnp.zeros(sums.shape, jnp.float32)
    for plane in range(planes):
        if plane % step_planes == 0:
            copies[plane // step_planes * 2].wait()
            copies[plane // step_planes * 2 + 1].wait()
        below = (plane - 1) % planes
        table[pl.ds(plane * rows * 4, rows, stride=4), :] = now[0, plane]
        table[pl.ds(plane * rows * 4 + 1, rows, stride=4), :] = now[1, plane]
        table[pl.ds(below * rows * 4 + 2, rows, stride=4), :] = now[0, plane]
        table[pl.ds(below * rows * 4 + 3, rows, stride=4), :] = now[1, plane]
    for copy in copies[2 * PARTS :] + indices + small:
        copy.wait()
    odd = odd_row()
    drops = DROP_DEV * lax.axis_size("gx")

    def edges(block):
        share = planes // 2 // count
        for number in range(share):
            for field in range(2):
                pair = block * share + number
                halves = []
                for half in range(2):
                    plane = pair * 2 + half
                    mixed = 1.5 * now[field, plane] - 0.5 * old[field, plane]
                    padded[field, plane, 8 : rows + 8, :] = mixed
                    top, bottom = mixed[0:2], mixed[rows - 2 : rows]
                    at = (field * planes + plane) * 2
                    facing[pl.ds(head_rows + at, 2), :] = jnp.where(odd, top, bottom)
                    backing[pl.ds(at, 2), :] = jnp.where(odd, bottom, top)
                    halves.append(mixed)
                turned = jnp.concatenate(halves, axis=0).T
                at = pl.multiple_of((field * (planes // 2) + pair) * 2 * rows, 2 * rows)
                head[:, pl.ds(at, 2 * rows)] = turned[0:2]
                tail[:, pl.ds(at, 2 * rows)] = turned[cols - 2 : cols]

    lane = iota((8, LANES), 1)
    live = tally[0, 0]
    sub = iota((8, LANES), 0)
    even = (sub & 1) == 0
    even_lane = (lane & 1) == 0

    def raw(block):
        blocks = []
        for half in range(2 * UNROLL):
            group = block * UNROLL + half // 2
            column = columns[pl.ds(pl.multiple_of((group * 2 + half % 2) * 8, 8), 8), :]
            found = jnp.zeros((8, LANES), jnp.float32)
            for j in range(HALF):
                at = (group, half % 2 * HALF + j)
                entry = pick(table[pl.ds(start[at], 8), :], column)
                found = jnp.where(lane >= 2 * j, entry, found)
            blocks.append(found)
        return blocks

    def refine(block, blocks, total):
        terms = []
        tables = []
        for unit in range(UNROLL):
            group = block * UNROLL + unit
            corner = factors[pl.ds(group, 8, stride=groups), :]
            corner = jnp.where(
                (sub == 2) | (sub == 3),
                pltpu.roll(corner, 6, 0),
                jnp.where((sub == 4) | (sub == 5), pltpu.roll(corner, 2, 0), corner),
            )
            other = swap_rows(corner, even)
            area = jnp.broadcast_to(surface[pl.ds(group, 1), :], (8, LANES))
            area = jnp.where(lane + group * LANES < live, area, 0.0)
            values = []
            for half in range(2):
                spread = (lane >> 1) + half * HALF
                weight = jnp.where(even_lane == even, pick(corner, spread), pick(other, spread))
                value = blocks[2 * unit + half] * weight
                value = value + pltpu.roll(value, 2, 0)
                value = value + pltpu.roll(value, 4, 0)
                value = value + jnp.where(even_lane, pltpu.roll(value, 127, 1), pltpu.roll(value, 1, 1))
                at = pl.ds(pl.multiple_of((group * 2 + half) * 8, 8), 8)
                scaled[at, :] = weight * pick(area, spread)
                fronts[at, :] = jnp.where(even, value, value - 0.5 * pltpu.roll(value, 1, 0))
                values.append(pick(value, (lane * 2) & 127))
            value = jnp.where(lane < HALF, values[0], values[1])
            term = jnp.where(sub == 2, 1.0, value) * area
            high = term.astype(jnp.bfloat16).astype(jnp.float32)
            terms.append(jnp.concatenate([high, term - high], axis=0).astype(jnp.bfloat16))
            label = jnp.broadcast_to(owner[pl.ds(group, 1), :], (drops, LANES))
            tables.append((label == iota((drops, LANES), 0)).astype(jnp.float32).astype(jnp.bfloat16))
        return total + lax.dot_general(
            jnp.concatenate(terms, axis=1),
            jnp.concatenate(tables, axis=1),
            (((1,), (1,)), ((), ())),
            preferred_element_type=jnp.float32,
        )

    def step(block, carry):
        total, *blocks = carry
        later = raw(block)
        edges(block - 1)
        return (refine(block - 1, blocks, total), *later)

    carry = (jnp.zeros((16, drops), jnp.float32), *raw(0))
    total, *blocks = lax.fori_loop(1, count, step, carry)
    edges(count - 1)
    total = refine(count - 1, blocks, total)
    total = total[0:8] + total[8:16]
    for number, at in enumerate(range(0, drops, LANES)):
        size = min(LANES, drops - at)
        facing[8 * number : 8 * number + 8, 0:size] = total[:, at : at + size]
        sums[8 * number : 8 * number + 8, 0:size] = total[:, at : at + size]
    for copy in later:
        copy.wait()


def prepare(halos, padded, side):
    facing, backing, left, right = halos
    planes, rows, cols = padded.shape[1], padded.shape[2] - 16, padded.shape[3]
    head_rows = facing.shape[0] - backing.shape[0]
    odd = odd_row()
    for field in range(2):
        for plane in range(planes):
            at = (field * planes + plane) * 2
            near = facing[head_rows + at : head_rows + at + 2, :]
            far = backing[at : at + 2, :]
            padded[field, plane, 6:8, :] = jnp.where(odd, near, far)
            padded[field, plane, rows + 8 : rows + 10, :] = jnp.where(odd, far, near)
        for pair in range(planes // 2):
            at = (field * (planes // 2) + pair) * 2 * rows
            block = jnp.concatenate(
                [
                    right[:, pl.ds(at, 2 * rows)],
                    jnp.zeros((cols - 4, 2 * rows), jnp.float32),
                    left[:, pl.ds(at, 2 * rows)],
                ],
                axis=0,
            )
            side[pl.ds(at, 2 * rows), :] = block.T


def advance(plane, now, speed, padded, side, outs):
    planes, rows, cols = now.shape[1:]
    lane = iota((rows, cols), 1)
    fraction = increment_span / 12.0
    speeds = [speed[k, plane].astype(jnp.float32) * fraction for k in range(3)]
    for field in range(2):
        center = padded[field, plane, 8 : rows + 8, :]
        edge = side[pl.ds(pl.multiple_of((field * planes + plane) * rows, rows), rows), :]
        wrap = lambda shift: padded[field, lax.rem(plane + shift + planes, planes), 8 : rows + 8, :]
        shift = lambda by: padded[field, plane, 8 + by : rows + 8 + by, :]
        around = [
            (wrap(1), wrap(2), wrap(-1), wrap(-2)),
            (shift(1), shift(2), shift(-1), shift(-2)),
            (
                pltpu.roll(jnp.where(lane < 1, edge, center), cols - 1, 1),
                pltpu.roll(jnp.where(lane < 2, edge, center), cols - 2, 1),
                pltpu.roll(jnp.where(lane >= cols - 1, edge, center), 1, 1),
                pltpu.roll(jnp.where(lane >= cols - 2, edge, center), 2, 1),
            ),
        ]
        near = 0.0
        far = 0.0
        total = now[field, plane] - (90.0 * diffusivity * fraction) * center
        for k, (ahead_one, ahead_two, behind_one, behind_two) in enumerate(around):
            near = near + (ahead_one + behind_one)
            far = far + (ahead_two + behind_two)
            total = total - speeds[k] * (8.0 * (ahead_one - behind_one) - (ahead_two - behind_two))
        outs[field][plane] = total + (diffusivity * fraction) * (16.0 * near - far)


def scatter_kernel(
    start,
    back,
    owner,
    scaled,
    fronts,
    now,
    padded,
    speed,
    sums,
    facing,
    backing,
    left,
    right,
    out_moist,
    out_warm,
    padded_out,
    side,
    result,
    begin,
    turn,
    arrived,
    *banks,
):
    planes, rows, cols = now.shape[1:]
    groups = owner.shape[0]
    size = banks[0].shape[0]
    step_planes = planes // PARTS
    slots = list(range(arrived.shape[0]))
    indices = [fetch(start, begin, arrived, slots), fetch(back, turn, arrived, slots)]
    outs = (result.at[0], result.at[1])

    def clear(step, carry):
        for bank in banks:
            bank[pl.ds(pl.multiple_of(step * 128, 128), 128), :] = jnp.zeros((128, cols), jnp.float32)
        return carry

    lax.fori_loop(0, size // 128, clear, 0)
    pieces = []
    for at in range(0, sums.shape[0], 8):
        totals = sums[at : at + 8, :]
        drop_vapour = totals[0:1] / totals[2:3]
        drop_warmth = totals[1:2] / totals[2:3]
        saturated = 0.5 * jnp.exp(saturation_rate * (drop_warmth - 1.0))
        for_mass = 2.0 * saturated - drop_vapour
        for_heat = drop_warmth - 0.5 * for_mass
        wide = (8, LANES)
        pieces.append(
            jnp.where(
                (iota(wide, 0) & 1) == 0,
                jnp.broadcast_to(for_mass, wide),
                jnp.broadcast_to(for_heat, wide),
            )
        )
    prepare((facing, backing, left, right), padded_out, side)
    for copy in indices:
        copy.wait()
    lane = iota((8, LANES), 1)

    def ready(block):
        values = []
        for unit in range(UNROLL):
            group = block * UNROLL + unit
            label = jnp.broadcast_to(owner[pl.ds(group, 1), :], (8, LANES))
            looked = pick(pieces[0], label & 127)
            for number in range(1, len(pieces)):
                looked = jnp.where(label >= number * LANES, pick(pieces[number], label & 127), looked)
            for half in range(2):
                at = pl.ds(pl.multiple_of((group * 2 + half) * 8, 8), 8)
                values.append(scaled[at, :] * (pick(looked, (lane >> 1) + half * HALF) - fronts[at, :]))
        return values

    def spill(block, values):
        for half in range(2 * UNROLL):
            for j in range(HALF):
                at = (block * UNROLL + half // 2, half % 2 * HALF + j)
                entry = jnp.where((lane >> 1) == j, values[half], 0.0)
                banks[j % len(banks)][pl.ds(begin[at], 8), :] += pltpu.roll(entry, turn[at], 1)

    def grid_share(block):
        for number in range(planes // count):
            advance(block * (planes // count) + number, now, speed, padded_out, side, outs)

    def step(block, values):
        later = ready(block + 1)
        grid_share(block)
        spill(block, values)
        return tuple(later)

    count = groups // UNROLL
    values = lax.fori_loop(0, count - 1, step, tuple(ready(0)))
    grid_share(count - 1)
    spill(count - 1, values)
    finished = []
    for plane in range(planes):
        before = (plane - 1) % planes
        for field, out in enumerate(outs):
            total = out[plane]
            for bank in banks:
                total = total + bank[pl.ds(plane * rows * 4 + field, rows, stride=4), :]
                total = total + bank[pl.ds(before * rows * 4 + 2 + field, rows, stride=4), :]
            out[plane] = total
        if (plane + 1) % step_planes == 0:
            span = pl.ds(plane + 1 - step_planes, step_planes)
            for out, target in zip(outs, (out_moist, out_warm)):
                finished.append(fetch(out.at[span], target.at[span], arrived, slots))
    for copy in finished:
        copy.wait()


def params(megabytes=40):
    return pltpu.CompilerParams(vmem_limit_bytes=int(megabytes * 1024) << 10)


def shards(
    gas_moisture,
    gas_warmth,
    prior_moisture,
    prior_warmth,
    flow_speeds,
    lower_base_cell,
    trilinear_factors,
    panel_surface,
    panel_owner,
    active_panel_tally,
):
    planes, rows, cols = gas_moisture.shape
    drops = DROP_DEV * lax.axis_size("gx")
    count = panel_surface.shape[1]
    groups = count // LANES
    f32 = jnp.float32
    shape = jax.ShapeDtypeStruct
    base = lower_base_cell.reshape(3 * groups, LANES)
    factors = trilinear_factors.reshape(8 * groups, LANES)
    surface = panel_surface.reshape(groups, LANES)
    owner = panel_owner.reshape(groups, LANES)
    field = shape((planes, rows, cols), f32)

    head_rows = -(-drops // LANES) * 8
    edge_rows = 2 * planes * 2
    spots = shape((groups, LANES), jnp.int32)
    trays = shape((2 * groups * 8, LANES), f32)
    pair = shape((2, planes, rows, cols), f32)
    wide = shape((2, planes, rows + 16, cols), f32)
    edge = shape((2, 2 * planes * rows), f32)
    inputs = (
        base,
        gas_moisture,
        gas_warmth,
        prior_moisture,
        prior_warmth,
        factors,
        surface,
        owner,
        flow_speeds,
    )
    start, back, label, scaled, fronts, now, blend, speed, sums, facing, backing, head, tail = pl.pallas_call(
        gather_kernel,
        out_shape=(
            spots,
            spots,
            spots,
            trays,
            trays,
            pair,
            wide,
            shape(flow_speeds.shape, jnp.bfloat16),
            shape((head_rows, cols), f32),
            shape((head_rows + edge_rows, cols), f32),
            shape((edge_rows, cols), f32),
            edge,
            edge,
        ),
        in_specs=[SMEM] + [HBM] * 9,
        out_specs=[VMEM] * 13,
        scratch_shapes=[
            pltpu.VMEM(base.shape, jnp.int32),
            pltpu.VMEM(factors.shape, f32),
            pltpu.VMEM(surface.shape, f32),
            pltpu.VMEM((planes * rows * 4 + 8, cols), f32),
            pltpu.VMEM(pair.shape, f32),
            pltpu.VMEM(trays.shape, jnp.int32),
            pltpu.SMEM(spots.shape, jnp.int32),
            pltpu.SemaphoreType.DMA((4 * PARTS + 9,)),
        ],
        compiler_params=params(GATHER_MB),
        name="gather",
    )(active_panel_tally, *[pltpu.with_memory_space_constraint(x, pltpu.HBM) for x in inputs])

    def permute(x, axis, target):
        size = lax.axis_size(axis)
        return lax.ppermute(x, axis, [(i, target(i, size)) for i in range(size)])

    got_facing = permute(facing, "gx", lambda i, n: i ^ 1)
    got_backing = permute(backing, "gx", lambda i, n: (i - 1 if i % 2 == 0 else i + 1) % n)
    from_left = permute(tail, "gy", lambda i, n: (i + 1) % n)
    from_right = permute(head, "gy", lambda i, n: (i - 1) % n)
    totals = sums + got_facing[0:head_rows]
    size = lax.axis_size("gx")
    stride = 2
    while stride < size:
        if size % (2 * stride) == 0:
            totals = totals + permute(totals, "gx", lambda i, n: i ^ stride)
            stride *= 2
        else:
            partial = totals
            for number in range(1, size // stride):
                totals = totals + permute(
                    partial, "gx", lambda i, n: (i + number * stride) % n
                )
            stride = size

    size = planes * rows * 4 + 128
    return pl.pallas_call(
        scatter_kernel,
        out_shape=(field, field, wide),
        in_specs=[VMEM] * 13,
        out_specs=[HBM] * 2 + [VMEM],
        input_output_aliases={6: 2},
        scratch_shapes=[
            pltpu.VMEM((2 * planes * rows, cols), f32),
            pltpu.VMEM(pair.shape, f32),
            pltpu.SMEM(spots.shape, jnp.int32),
            pltpu.SMEM(spots.shape, jnp.int32),
            pltpu.SemaphoreType.DMA((2 * PARTS + 2,)),
        ]
        + [pltpu.VMEM((size, cols), f32)] * COPIES,
        compiler_params=params(SCATTER_MB),
        name="scatter",
    )(
        start,
        back,
        label,
        scaled,
        fronts,
        now,
        blend,
        speed,
        totals,
        got_facing,
        got_backing,
        from_left,
        from_right,
    )[:2]


def solution(mesh):
    return jax.shard_map(
        shards,
        mesh=mesh,
        in_specs=(
            P(None, "gx", "gy"),
            P(None, "gx", "gy"),
            P(None, "gx", "gy"),
            P(None, "gx", "gy"),
            P(None, None, "gx", "gy"),
            P(None, "gy", "gx"),
            P(None, "gy", "gx"),
            P("gy", "gx"),
            P("gy", "gx"),
            P("gy", "gx"),
        ),
        out_specs=(P(None, "gx", "gy"), P(None, "gx", "gy")),
        check_vma=False,
    )
```

```python
import functools

import jax
import jax.numpy as jnp
from jax import lax
from jax.experimental import pallas as pl
from jax.experimental.pallas import tpu as pltpu
from jax.sharding import PartitionSpec as P

DROP_DEV = 20
LANES = 128
HALF = 64

increment_span = 0.1
diffusivity = 1.0
mass_rate = 2.0
saturation_rate = 2.0
thermal_flux = 1.0
enthalpy_evaporation = 0.5

VMEM = pl.BlockSpec(memory_space=pltpu.VMEM)
HBM = pl.BlockSpec(memory_space=pltpu.HBM)
SMEM = pl.BlockSpec(memory_space=pltpu.SMEM)
COPIES = 4
UNROLL = 8
GATHER_MB = 24
SCATTER_MB = 20
PARTS = 4


def iota(shape, dim):
    return lax.broadcasted_iota(jnp.int32, shape, dim)


def pick(values, index):
    return jnp.take_along_axis(values, index, axis=1, mode="promise_in_bounds")


def swap_rows(x, even):
    return jnp.where(even, pltpu.roll(x, 7, 0), pltpu.roll(x, 1, 0))


def odd_row():
    return (lax.axis_index("gx") & 1) == 1


def fetch(source, target, arrived, slots):
    copy = pltpu.make_async_copy(source, target, arrived.at[slots.pop()])
    copy.start()
    return copy


def gather_kernel(
    tally,
    base_in,
    moist,
    warm,
    old_moist,
    old_warm,
    factors_in,
    surface_in,
    owner_in,
    speed_in,
    start_out,
    back_out,
    owner,
    scaled,
    fronts,
    now,
    padded,
    speed,
    sums,
    facing,
    backing,
    head,
    tail,
    base,
    factors,
    surface,
    table,
    old,
    columns,
    start,
    arrived,
):
    planes, rows, cols = moist.shape
    groups = surface.shape[0]
    count = groups // UNROLL
    head_rows = facing.shape[0] - backing.shape[0]
    step_planes = planes // PARTS
    slots = list(range(arrived.shape[0]))
    first = fetch(base_in, base, arrived, slots)
    copies = []
    for levels in ((0, 2), (1, 3)):
        for part in range(PARTS):
            for level in levels:
                span = pl.ds(part * step_planes, step_planes)
                source = (moist, old_moist, warm, old_warm)[level]
                target = (now, old)[level % 2].at[level // 2, span]
                copies.append(fetch(source.at[span], target, arrived, slots))
    small = [
        fetch(source, target, arrived, slots)
        for source, target in (
            (factors_in, factors),
            (surface_in, surface),
            (owner_in, owner),
        )
    ]
    later = [fetch(speed_in.at[k], speed.at[k], arrived, slots) for k in range(3)]
    first.wait()
    spot = (groups, LANES)
    column = base[2 * groups : 3 * groups, :] - lax.axis_index("gy") * cols
    row = base[groups : 2 * groups, :] - lax.axis_index("gx") * rows
    lane = iota((8, LANES), 1)
    for group in range(groups):
        wide = jnp.broadcast_to(column[group : group + 1], (8, LANES))
        for half in range(2):
            columns[(2 * group + half) * 8 : (2 * group + half) * 8 + 8, :] = (
                pick(wide, (lane >> 1) + half * HALF) + (lane & 1)
            )
    back_out[...] = (column - 2 * (iota(spot, 1) & (HALF - 1))) & 127
    start_out[...] = (base[0:groups, :] * rows + row) * 4
    indices = [fetch(start_out, start, arrived, slots)]
    facing[0:head_rows, :] = jnp.zeros((head_rows, LANES), jnp.float32)
    sums[...] = jnp.zeros(sums.shape, jnp.float32)
    for plane in range(planes):
        if plane % step_planes == 0:
            copies[plane // step_planes * 2].wait()
            copies[plane // step_planes * 2 + 1].wait()
        below = (plane - 1) % planes
        table[pl.ds(plane * rows * 4, rows, stride=4), :] = now[0, plane]
        table[pl.ds(plane * rows * 4 + 1, rows, stride=4), :] = now[1, plane]
        table[pl.ds(below * rows * 4 + 2, rows, stride=4), :] = now[0, plane]
        table[pl.ds(below * rows * 4 + 3, rows, stride=4), :] = now[1, plane]
    for copy in copies[2 * PARTS :] + indices + small:
        copy.wait()
    odd = odd_row()
    drops = DROP_DEV * lax.axis_size("gx")

    def edges(block):
        share = planes // 2 // count
        for number in range(share):
            for field in range(2):
                pair = block * share + number
                halves = []
                for half in range(2):
                    plane = pair * 2 + half
                    mixed = 1.5 * now[field, plane] - 0.5 * old[field, plane]
                    padded[field, plane, 8 : rows + 8, :] = mixed
                    top, bottom = mixed[0:2], mixed[rows - 2 : rows]
                    at = (field * planes + plane) * 2
                    facing[pl.ds(head_rows + at, 2), :] = jnp.where(odd, top, bottom)
                    backing[pl.ds(at, 2), :] = jnp.where(odd, bottom, top)
                    halves.append(mixed)
                turned = jnp.concatenate(halves, axis=0).T
                at = pl.multiple_of((field * (planes // 2) + pair) * 2 * rows, 2 * rows)
                head[:, pl.ds(at, 2 * rows)] = turned[0:2]
                tail[:, pl.ds(at, 2 * rows)] = turned[cols - 2 : cols]

    lane = iota((8, LANES), 1)
    live = tally[0, 0]
    sub = iota((8, LANES), 0)
    even = (sub & 1) == 0
    even_lane = (lane & 1) == 0

    def raw(block):
        blocks = []
        for half in range(2 * UNROLL):
            group = block * UNROLL + half // 2
            column = columns[pl.ds(pl.multiple_of((group * 2 + half % 2) * 8, 8), 8), :]
            found = jnp.zeros((8, LANES), jnp.float32)
            for j in range(HALF):
                at = (group, half % 2 * HALF + j)
                entry = pick(table[pl.ds(start[at], 8), :], column)
                found = jnp.where(lane >= 2 * j, entry, found)
            blocks.append(found)
        return blocks

    def refine(block, blocks, total):
        terms = []
        tables = []
        for unit in range(UNROLL):
            group = block * UNROLL + unit
            corner = factors[pl.ds(group, 8, stride=groups), :]
            corner = jnp.where(
                (sub == 2) | (sub == 3),
                pltpu.roll(corner, 6, 0),
                jnp.where((sub == 4) | (sub == 5), pltpu.roll(corner, 2, 0), corner),
            )
            other = swap_rows(corner, even)
            area = jnp.broadcast_to(surface[pl.ds(group, 1), :], (8, LANES))
            area = jnp.where(lane + group * LANES < live, area, 0.0)
            values = []
            for half in range(2):
                spread = (lane >> 1) + half * HALF
                weight = jnp.where(even_lane == even, pick(corner, spread), pick(other, spread))
                value = blocks[2 * unit + half] * weight
                value = value + pltpu.roll(value, 2, 0)
                value = value + pltpu.roll(value, 4, 0)
                value = value + jnp.where(even_lane, pltpu.roll(value, 127, 1), pltpu.roll(value, 1, 1))
                at = pl.ds(pl.multiple_of((group * 2 + half) * 8, 8), 8)
                scaled[at, :] = weight * pick(area, spread)
                fronts[at, :] = jnp.where(even, value, value - 0.5 * pltpu.roll(value, 1, 0))
                values.append(pick(value, (lane * 2) & 127))
            value = jnp.where(lane < HALF, values[0], values[1])
            term = jnp.where(sub == 2, 1.0, value) * area
            high = term.astype(jnp.bfloat16).astype(jnp.float32)
            terms.append(jnp.concatenate([high, term - high], axis=0).astype(jnp.bfloat16))
            label = jnp.broadcast_to(owner[pl.ds(group, 1), :], (drops, LANES))
            tables.append((label == iota((drops, LANES), 0)).astype(jnp.float32).astype(jnp.bfloat16))
        return total + lax.dot_general(
            jnp.concatenate(terms, axis=1),
            jnp.concatenate(tables, axis=1),
            (((1,), (1,)), ((), ())),
            preferred_element_type=jnp.float32,
        )

    def step(block, carry):
        total, *blocks = carry
        later = raw(block)
        edges(block - 1)
        return (refine(block - 1, blocks, total), *later)

    carry = (jnp.zeros((16, drops), jnp.float32), *raw(0))
    total, *blocks = lax.fori_loop(1, count, step, carry)
    edges(count - 1)
    total = refine(count - 1, blocks, total)
    total = total[0:8] + total[8:16]
    for number, at in enumerate(range(0, drops, LANES)):
        size = min(LANES, drops - at)
        facing[8 * number : 8 * number + 8, 0:size] = total[:, at : at + size]
        sums[8 * number : 8 * number + 8, 0:size] = total[:, at : at + size]
    for copy in later:
        copy.wait()


def prepare(halos, padded, side):
    facing, backing, left, right = halos
    planes, rows, cols = padded.shape[1], padded.shape[2] - 16, padded.shape[3]
    head_rows = facing.shape[0] - backing.shape[0]
    odd = odd_row()
    for field in range(2):
        for plane in range(planes):
            at = (field * planes + plane) * 2
            near = facing[head_rows + at : head_rows + at + 2, :]
            far = backing[at : at + 2, :]
            padded[field, plane, 6:8, :] = jnp.where(odd, near, far)
            padded[field, plane, rows + 8 : rows + 10, :] = jnp.where(odd, far, near)
        for pair in range(planes // 2):
            at = (field * (planes // 2) + pair) * 2 * rows
            block = jnp.concatenate(
                [
                    right[:, pl.ds(at, 2 * rows)],
                    jnp.zeros((cols - 4, 2 * rows), jnp.float32),
                    left[:, pl.ds(at, 2 * rows)],
                ],
                axis=0,
            )
            side[pl.ds(at, 2 * rows), :] = block.T


def advance(plane, now, speed, padded, side, outs):
    planes, rows, cols = now.shape[1:]
    lane = iota((rows, cols), 1)
    fraction = increment_span / 12.0
    speeds = [speed[k, plane].astype(jnp.float32) * fraction for k in range(3)]
    for field in range(2):
        center = padded[field, plane, 8 : rows + 8, :]
        edge = side[pl.ds(pl.multiple_of((field * planes + plane) * rows, rows), rows), :]
        wrap = lambda shift: padded[field, lax.rem(plane + shift + planes, planes), 8 : rows + 8, :]
        shift = lambda by: padded[field, plane, 8 + by : rows + 8 + by, :]
        around = [
            (wrap(1), wrap(2), wrap(-1), wrap(-2)),
            (shift(1), shift(2), shift(-1), shift(-2)),
            (
                pltpu.roll(jnp.where(lane < 1, edge, center), cols - 1, 1),
                pltpu.roll(jnp.where(lane < 2, edge, center), cols - 2, 1),
                pltpu.roll(jnp.where(lane >= cols - 1, edge, center), 1, 1),
                pltpu.roll(jnp.where(lane >= cols - 2, edge, center), 2, 1),
            ),
        ]
        near = 0.0
        far = 0.0
        total = now[field, plane] - (90.0 * diffusivity * fraction) * center
        for k, (ahead_one, ahead_two, behind_one, behind_two) in enumerate(around):
            near = near + (ahead_one + behind_one)
            far = far + (ahead_two + behind_two)
            total = total - speeds[k] * (8.0 * (ahead_one - behind_one) - (ahead_two - behind_two))
        outs[field][plane] = total + (diffusivity * fraction) * (16.0 * near - far)


def scatter_kernel(
    start,
    back,
    owner,
    scaled,
    fronts,
    now,
    padded,
    speed,
    sums,
    facing,
    backing,
    left,
    right,
    out_moist,
    out_warm,
    padded_out,
    side,
    result,
    begin,
    turn,
    arrived,
    *banks,
):
    planes, rows, cols = now.shape[1:]
    groups = owner.shape[0]
    size = banks[0].shape[0]
    step_planes = planes // PARTS
    slots = list(range(arrived.shape[0]))
    indices = [fetch(start, begin, arrived, slots), fetch(back, turn, arrived, slots)]
    outs = (result.at[0], result.at[1])

    def clear(step, carry):
        for bank in banks:
            bank[pl.ds(pl.multiple_of(step * 128, 128), 128), :] = jnp.zeros((128, cols), jnp.float32)
        return carry

    lax.fori_loop(0, size // 128, clear, 0)
    pieces = []
    for at in range(0, sums.shape[0], 8):
        totals = sums[at : at + 8, :]
        drop_vapour = totals[0:1] / totals[2:3]
        drop_warmth = totals[1:2] / totals[2:3]
        saturated = 0.5 * jnp.exp(saturation_rate * (drop_warmth - 1.0))
        for_mass = 2.0 * saturated - drop_vapour
        for_heat = drop_warmth - 0.5 * for_mass
        wide = (8, LANES)
        pieces.append(
            jnp.where(
                (iota(wide, 0) & 1) == 0,
                jnp.broadcast_to(for_mass, wide),
                jnp.broadcast_to(for_heat, wide),
            )
        )
    prepare((facing, backing, left, right), padded_out, side)
    for copy in indices:
        copy.wait()
    lane = iota((8, LANES), 1)

    def ready(block):
        values = []
        for unit in range(UNROLL):
            group = block * UNROLL + unit
            label = jnp.broadcast_to(owner[pl.ds(group, 1), :], (8, LANES))
            looked = pick(pieces[0], label & 127)
            for number in range(1, len(pieces)):
                looked = jnp.where(label >= number * LANES, pick(pieces[number], label & 127), looked)
            for half in range(2):
                at = pl.ds(pl.multiple_of((group * 2 + half) * 8, 8), 8)
                values.append(scaled[at, :] * (pick(looked, (lane >> 1) + half * HALF) - fronts[at, :]))
        return values

    def spill(block, values):
        for half in range(2 * UNROLL):
            for j in range(HALF):
                at = (block * UNROLL + half // 2, half % 2 * HALF + j)
                entry = jnp.where((lane >> 1) == j, values[half], 0.0)
                banks[j % len(banks)][pl.ds(begin[at], 8), :] += pltpu.roll(entry, turn[at], 1)

    def grid_share(block):
        for number in range(planes // count):
            advance(block * (planes // count) + number, now, speed, padded_out, side, outs)

    def step(block, values):
        later = ready(block + 1)
        grid_share(block)
        spill(block, values)
        return tuple(later)

    count = groups // UNROLL
    values = lax.fori_loop(0, count - 1, step, tuple(ready(0)))
    grid_share(count - 1)
    spill(count - 1, values)
    finished = []
    for plane in range(planes):
        before = (plane - 1) % planes
        for field, out in enumerate(outs):
            total = out[plane]
            for bank in banks:
                total = total + bank[pl.ds(plane * rows * 4 + field, rows, stride=4), :]
                total = total + bank[pl.ds(before * rows * 4 + 2 + field, rows, stride=4), :]
            out[plane] = total
        if (plane + 1) % step_planes == 0:
            span = pl.ds(plane + 1 - step_planes, step_planes)
            for out, target in zip(outs, (out_moist, out_warm)):
                finished.append(fetch(out.at[span], target.at[span], arrived, slots))
    for copy in finished:
        copy.wait()


def params(megabytes=40):
    return pltpu.CompilerParams(vmem_limit_bytes=int(megabytes * 1024) << 10)


def shards(
    gas_moisture,
    gas_warmth,
    prior_moisture,
    prior_warmth,
    flow_speeds,
    lower_base_cell,
    trilinear_factors,
    panel_surface,
    panel_owner,
    active_panel_tally,
):
    planes, rows, cols = gas_moisture.shape
    drops = DROP_DEV * lax.axis_size("gx")
    count = panel_surface.shape[1]
    groups = count // LANES
    f32 = jnp.float32
    shape = jax.ShapeDtypeStruct
    base = lower_base_cell.reshape(3 * groups, LANES)
    factors = trilinear_factors.reshape(8 * groups, LANES)
    surface = panel_surface.reshape(groups, LANES)
    owner = panel_owner.reshape(groups, LANES)
    field = shape((planes, rows, cols), f32)

    head_rows = -(-drops // LANES) * 8
    edge_rows = 2 * planes * 2
    spots = shape((groups, LANES), jnp.int32)
    trays = shape((2 * groups * 8, LANES), f32)
    pair = shape((2, planes, rows, cols), f32)
    wide = shape((2, planes, rows + 16, cols), f32)
    edge = shape((2, 2 * planes * rows), f32)
    inputs = (
        base,
        gas_moisture,
        gas_warmth,
        prior_moisture,
        prior_warmth,
        factors,
        surface,
        owner,
        flow_speeds,
    )
    start, back, label, scaled, fronts, now, blend, speed, sums, facing, backing, head, tail = pl.pallas_call(
        gather_kernel,
        out_shape=(
            spots,
            spots,
            spots,
            trays,
            trays,
            pair,
            wide,
            shape(flow_speeds.shape, jnp.bfloat16),
            shape((head_rows, cols), f32),
            shape((head_rows + edge_rows, cols), f32),
            shape((edge_rows, cols), f32),
            edge,
            edge,
        ),
        in_specs=[SMEM] + [HBM] * 9,
        out_specs=[VMEM] * 13,
        scratch_shapes=[
            pltpu.VMEM(base.shape, jnp.int32),
            pltpu.VMEM(factors.shape, f32),
            pltpu.VMEM(surface.shape, f32),
            pltpu.VMEM((planes * rows * 4 + 8, cols), f32),
            pltpu.VMEM(pair.shape, f32),
            pltpu.VMEM(trays.shape, jnp.int32),
            pltpu.SMEM(spots.shape, jnp.int32),
            pltpu.SemaphoreType.DMA((4 * PARTS + 9,)),
        ],
        compiler_params=params(GATHER_MB),
        name="gather",
    )(active_panel_tally, *[pltpu.with_memory_space_constraint(x, pltpu.HBM) for x in inputs])

    def permute(x, axis, target):
        size = lax.axis_size(axis)
        return lax.ppermute(x, axis, [(i, target(i, size)) for i in range(size)])

    got_facing = permute(facing, "gx", lambda i, n: i ^ 1)
    got_backing = permute(backing, "gx", lambda i, n: (i - 1 if i % 2 == 0 else i + 1) % n)
    from_left = permute(tail, "gy", lambda i, n: (i + 1) % n)
    from_right = permute(head, "gy", lambda i, n: (i - 1) % n)
    totals = sums + got_facing[0:head_rows]
    size = lax.axis_size("gx")
    stride = 2
    while stride < size:
        if size % (2 * stride) == 0:
            totals = totals + permute(totals, "gx", lambda i, n: i ^ stride)
            stride *= 2
        else:
            partial = totals
            for number in range(1, size // stride):
                totals = totals + permute(
                    partial, "gx", lambda i, n: (i + number * stride) % n
                )
            stride = size

    size = planes * rows * 4 + 128
    return pl.pallas_call(
        scatter_kernel,
        out_shape=(field, field, wide),
        in_specs=[VMEM] * 13,
        out_specs=[HBM] * 2 + [VMEM],
        input_output_aliases={6: 2},
        scratch_shapes=[
            pltpu.VMEM((2 * planes * rows, cols), f32),
            pltpu.VMEM(pair.shape, f32),
            pltpu.SMEM(spots.shape, jnp.int32),
            pltpu.SMEM(spots.shape, jnp.int32),
            pltpu.SemaphoreType.DMA((2 * PARTS + 2,)),
        ]
        + [pltpu.VMEM((size, cols), f32)] * COPIES,
        compiler_params=params(SCATTER_MB),
        name="scatter",
    )(
        start,
        back,
        label,
        scaled,
        fronts,
        now,
        blend,
        speed,
        totals,
        got_facing,
        got_backing,
        from_left,
        from_right,
    )[:2]


def solution(mesh):
    return jax.shard_map(
        shards,
        mesh=mesh,
        in_specs=(
            P(None, "gx", "gy"),
            P(None, "gx", "gy"),
            P(None, "gx", "gy"),
            P(None, "gx", "gy"),
            P(None, None, "gx", "gy"),
            P(None, "gy", "gx"),
            P(None, "gy", "gx"),
            P("gy", "gx"),
            P("gy", "gx"),
            P("gy", "gx"),
        ),
        out_specs=(P(None, "gx", "gy"), P(None, "gx", "gy")),
        check_vma=False,
    )
```
